32 devices in a mesh: gx: 8 (over y, x, core), gy: 4 (over z).
Axes of the slice: x: 2, y: 2, z: 4, core: 2. Of those that a mesh axis runs over, the one named last changes fastest.
Arguments:
- ends: float32 [6, 262144], P(None, ('gx', 'gy')), may hold values from -0.05 to 1.05, as said below
- burgers: float32 [3, 262144], P(None, ('gx', 'gy')), may hold values from -4 to 4
- seg_cell: int32 [262144], P(('gx', 'gy')), may hold values from 0 to 255, as said below
- send_blocks: int32 [32, 4, 24], P(('gx', 'gy')), may hold values from 0 to 63
- send_count: int32 [32, 4], P(('gx', 'gy')), may hold values from 1 to 24, as said below
- pair_list: int32 [32, 64, 2], P(('gx', 'gy')), may hold values from 0 to 159, as said below
- pair_count: int32 [32], replicated, may hold values from 16 to 64, as said below
Outputs:
- end_force: float32 [6, 262144], P(None, ('gx', 'gy'))
The draws below stay inside these ranges and needn't reach their ends.
Inputs may be any that keep to these rules, and one draw needn't show every extreme that they name: `ends`: each segment's midpoint lies inside the coarse cell seg_cell names and inside its own domain's region. `seg_cell`: the coarse cell holding the segment's midpoint. `send_count`: every domain has a neighbour to which exactly 24 slots are used. `pair_list`: first entry a local block below 64; second an extended block; slots beyond the count are ignored. `pair_count`: some domain has exactly 64.
All inputs are finite; a program needn't handle non-finite values.
Results may differ from the reference program's by a relative error of at most 0.0003.
Values sent between devices are 32-bit elements; how exact they have to be, the bound alone decides.
A program may use at most 64 MiB of HBM per device.

```python
import jax
import jax.numpy as jnp
from jax import lax

SEG_DEV = 8192
GHOST = 24
PAIRS = 64
CELL_XY = 8
CELL_Z = 4
CELLS = 256
BLOCKS = 64
DOMX = 8
DOMY = 4
DOMAINS = 32
SEGS = 262144
N_GX = 8
N_GY = 4


def grid_index(key):
    key = jax.random.fold_in(key, 101)
    key_x, key_y, key_z = jax.random.split(key, 3)
    index = jnp.arange(SEGS, dtype=jnp.int32)
    domain = index // SEG_DEV
    fine_x = domain // DOMY * 4 + jax.random.randint(key_x, (SEGS,), 0, 4)
    fine_y = domain % DOMY * 4 + jax.random.randint(key_y, (SEGS,), 0, 4)
    fine_z = jax.random.randint(key_z, (SEGS,), 0, 4 * CELL_Z)
    return (fine_x, fine_y, fine_z)


def draw_ends(key, part):
    fine_x, fine_y, fine_z = grid_index(key)
    key = jax.random.fold_in(key, 1)
    key_a, key_b = jax.random.split(key)
    offset = jax.random.uniform(key_a, (3, SEGS), jnp.float32, 0.05, 0.95)
    mid = jnp.stack([(fine_x.astype(jnp.float32) + offset[0]) / (4 * DOMX), (fine_y.astype(jnp.float32) + offset[1]) / (4 * DOMY), (fine_z.astype(jnp.float32) + offset[2]) / (64 * CELL_Z)], 0)
    line = 0.01 * jnp.clip(jax.random.normal(key_b, (3, SEGS), jnp.float32), -4.0, 4.0)
    return jnp.concatenate([mid - 0.5 * line, mid + 0.5 * line], 0)


def draw_seg_cell(key, part):
    fine_x, fine_y, fine_z = grid_index(key)
    cell_x = fine_x * CELL_XY // (4 * DOMX)
    cell_y = fine_y * CELL_XY // (4 * DOMY)
    return ((cell_x * CELL_XY + cell_y) * CELL_Z + fine_z // 4).astype(jnp.int32)


def draw_send_count(key, part):
    key = jax.random.fold_in(key, 3)
    key_a, key_b = jax.random.split(key)
    counts = jax.random.randint(key_a, (DOMAINS, 4), 1, GHOST + 1)
    full = jax.random.randint(key_b, (DOMAINS,), 0, 4)
    return jnp.where(jnp.arange(4)[None, :] == full[:, None], GHOST, counts).astype(jnp.int32)


def draw_pair_list(key, part):
    key = jax.random.fold_in(key, 4)
    keys = jax.random.split(key, 5)
    first = jax.random.randint(keys[0], (DOMAINS, PAIRS), 0, BLOCKS)
    local = jax.random.randint(keys[1], (DOMAINS, PAIRS), 0, BLOCKS)
    ghost = BLOCKS + jax.random.randint(keys[2], (DOMAINS, PAIRS), 0, 4 * GHOST)
    coin = jax.random.randint(keys[3], (DOMAINS, PAIRS), 0, 2)
    second = jnp.where(coin == 1, ghost, local)
    top = jax.random.randint(keys[4], (), 0, DOMAINS)
    mark = (jnp.arange(DOMAINS)[:, None] == top) & (jnp.arange(PAIRS)[None, :] == 0)
    second = jnp.where(mark, BLOCKS + 4 * GHOST - 1, second)
    return jnp.stack([first, second], -1).astype(jnp.int32)


def draw_pair_count(key, part):
    key = jax.random.fold_in(key, 5)
    key_a, key_b = jax.random.split(key)
    counts = jax.random.randint(key_a, (DOMAINS,), PAIRS // 4, PAIRS + 1)
    busy = jax.random.randint(key_b, (), 0, DOMAINS)
    return jnp.where(jnp.arange(DOMAINS) == busy, PAIRS, counts).astype(jnp.int32)


def set_ends(result, key, low, largest):
    longest = result.shape.index(max(result.shape))
    spots = []
    for shift in (0, 1):
        where = [jax.random.randint(jax.random.fold_in(key, axis), (), 0, length) for axis, length in enumerate(result.shape)]
        where[longest] = (where[longest] + shift) % result.shape[longest]
        spots.append(tuple(where))
    return result.at[spots[0]].set(low).at[spots[1]].set(largest)


def levels(rng, dims, cuts, smallest, largest):
    def one(position, parts):
        draws = jax.random.uniform(jax.random.fold_in(jax.random.fold_in(rng, 6), position), (parts,), jnp.float32, smallest / len(cuts), largest / len(cuts))
        return jnp.repeat(jnp.exp(draws), dims[position] // parts).reshape((-1,) + (1,) * (len(dims) - position - 1))

    factor_of = one(*cuts[0])
    for cut in cuts[1:]:
        factor_of = factor_of * one(*cut)
    return factor_of


def centred(key, shape, scale, bound, pieces=(), kind=jnp.bfloat16):
    array = jax.random.normal(key, shape, jnp.float32) * scale
    if len(pieces) > 0:
        array = levels(key, shape, pieces, -0.22, 0.18) * array
    return jnp.clip(array, min=-bound, max=bound).astype(kind)


def setup_inputs(seed: int = 0) -> dict:
    seeds = jax.random.split(jax.random.key(seed), 8)
    ends = draw_ends(jax.random.fold_in(seeds[7], 71), 0)
    burgers = centred(seeds[1], (3, SEGS), 1.0, 4.0, ((1, 32),), jnp.float32)
    seg_cell = draw_seg_cell(jax.random.fold_in(seeds[7], 71), 0)
    send_blocks = set_ends(jax.random.randint(seeds[3], (DOMAINS, 4, GHOST), 0, BLOCKS), jax.random.fold_in(seeds[3], 1), 0, BLOCKS - 1).astype(jnp.int32)
    send_count = draw_send_count(jax.random.fold_in(seeds[7], 71), 0)
    pair_list = draw_pair_list(jax.random.fold_in(seeds[7], 71), 0)
    pair_count = draw_pair_count(jax.random.fold_in(seeds[7], 71), 0)
    return dict(ends=ends, burgers=burgers, seg_cell=seg_cell, send_blocks=send_blocks, send_count=send_count, pair_list=pair_list, pair_count=pair_count)


CORE_SQ = 2.5e-05
NEAR_COEF = 0.2
FAR_COEF = 0.2

def pair_forces(block_s, block_t, same):
    mid_s = 0.5 * (block_s[0:3] + block_s[3:6])
    line_s = block_s[3:6] - block_s[0:3]
    burg_s = block_s[6:9]
    mid_t = 0.5 * (block_t[0:3] + block_t[3:6])
    line_t = block_t[3:6] - block_t[0:3]
    burg_t = block_t[6:9]
    rel = mid_t[:, None, :] - mid_s[:, :, None]
    quad = lax.optimization_barrier(jnp.sum(rel * rel, 0)) + CORE_SQ
    inv = lax.rsqrt(quad)
    inv3 = inv * inv * inv
    dot_bb = lax.optimization_barrier(jnp.sum(burg_s[:, :, None] * burg_t[:, None, :], 0))
    dot_ll = lax.optimization_barrier(jnp.sum(line_s[:, :, None] * line_t[:, None, :], 0))
    dot_bl = lax.optimization_barrier(jnp.sum(burg_s[:, :, None] * line_t[:, None, :], 0))
    dot_lb = lax.optimization_barrier(jnp.sum(line_s[:, :, None] * burg_t[:, None, :], 0))
    lane = jnp.arange(128)
    upper = (lane[:, None] < lane[None, :]).astype(jnp.float32)
    keep = jnp.where(same > 0.5, upper, jnp.ones_like(upper))
    coef = NEAR_COEF * (dot_bb * dot_ll + dot_bl * dot_lb) * inv3 * keep
    push = coef[None] * rel
    len_s = lax.optimization_barrier(jnp.sum(line_s * line_s, 0))
    len_t = lax.optimization_barrier(jnp.sum(line_t * line_t, 0))
    share_s = 0.5 * lax.optimization_barrier(jnp.sum(line_s[:, :, None] * rel, 0)) / (quad + len_s[:, None])
    share_t = -0.5 * lax.optimization_barrier(jnp.sum(line_t[:, None, :] * rel, 0)) / (quad + len_t[None, :])
    first_s = -lax.optimization_barrier(jnp.sum((0.5 - share_s)[None] * push, 2))
    second_s = -lax.optimization_barrier(jnp.sum((0.5 + share_s)[None] * push, 2))
    first_t = lax.optimization_barrier(jnp.sum((0.5 - share_t)[None] * push, 1))
    second_t = lax.optimization_barrier(jnp.sum((0.5 + share_t)[None] * push, 1))
    return (jnp.concatenate([first_s, second_s], 0), jnp.concatenate([first_t, second_t], 0))

def near_loop(extended, pairs, start, stop, totals):

    def step(p, acc):
        left = pairs[p, 0]
        right = pairs[p, 1]
        same = (left == right).astype(jnp.float32)
        force_s, force_t = pair_forces(extended[left], extended[right], same)
        acc = acc.at[left].add(force_s)
        return acc.at[right].add(force_t)
    return lax.fori_loop(start, stop, step, totals)

def moment_terms(ends, burgers):
    line = ends[3:6] - ends[0:3]
    rows = [burgers[p] * line[q] for p in range(3) for q in range(3)]
    rows = rows + [line[q] for q in range(3)]
    return jnp.stack(rows, 0)

def cell_coords(cell):
    return (cell // (CELL_XY * CELL_Z), cell // CELL_Z % CELL_XY, cell % CELL_Z)

def far_field(ends, burgers, seg_cell, moments):
    count = ends.shape[1]
    width = min(512, count)
    groups = count // width
    ends_b = ends.reshape(6, groups, width).transpose(1, 0, 2)
    burg_b = burgers.reshape(3, groups, width).transpose(1, 0, 2)
    cell_b = seg_cell.reshape(groups, width)
    kid = jnp.arange(CELLS, dtype=jnp.int32)
    kx, ky, kz = cell_coords(kid)
    centre = jnp.stack([(kx.astype(jnp.float32) + 0.5) / CELL_XY, (ky.astype(jnp.float32) + 0.5) / CELL_XY, (kz.astype(jnp.float32) + 0.5) / (16 * CELL_Z)], 0)

    def one(item):
        block_e, block_b, block_c = item
        terms = moment_terms(block_e, block_b)
        weight = jnp.dot(terms.T, moments, precision=lax.Precision.HIGHEST)
        sx, sy, sz = cell_coords(block_c)
        gap = jnp.maximum(jnp.maximum(jnp.abs(kx[None, :] - sx[:, None]), jnp.abs(ky[None, :] - sy[:, None])), jnp.abs(kz[None, :] - sz[:, None]))
        distant = (gap >= 2).astype(jnp.float32)
        mid = 0.5 * (block_e[0:3] + block_e[3:6])
        rel = centre[:, None, :] - mid[:, :, None]
        quad = lax.optimization_barrier(jnp.sum(rel * rel, 0)) + CORE_SQ
        inv = lax.rsqrt(quad)
        coef = FAR_COEF * weight * inv * inv * inv * distant
        return lax.optimization_barrier(jnp.sum(coef[None] * rel, 2))
    out = lax.map(one, (ends_b, burg_b, cell_b))
    return out.transpose(1, 0, 2).reshape(3, count)

def shifted(arr, axis, by):
    size = arr.shape[axis]
    empty = jnp.zeros_like(lax.slice_in_dim(arr, 0, 1, axis=axis))
    if by > 0:
        return jnp.concatenate([empty, lax.slice_in_dim(arr, 0, size - 1, axis=axis)], axis)
    return jnp.concatenate([lax.slice_in_dim(arr, 1, size, axis=axis), empty], axis)

def reference(ends, burgers, seg_cell, send_blocks, send_count, pair_list, pair_count):
    domains = N_GX * N_GY
    blocks = SEG_DEV // 128
    width = GHOST
    data = jnp.concatenate([ends, burgers], 0).reshape(9, domains, blocks, 128).transpose(1, 2, 0, 3)
    slot_ok = (jnp.arange(width)[None, None, :] < send_count[:, :, None]).astype(jnp.float32)
    rows = jnp.arange(domains)[:, None, None]
    sent = data[rows, send_blocks] * slot_ok[..., None, None]
    grid = sent.reshape(N_GX, N_GY, 4, width, 9, 128)
    ghosts = jnp.stack([shifted(grid[:, :, 1], 0, 1), shifted(grid[:, :, 0], 0, -1), shifted(grid[:, :, 3], 1, 1), shifted(grid[:, :, 2], 1, -1)], 2)
    extended = jnp.concatenate([data, ghosts.reshape(domains, 4 * width, 9, 128)], 1)

    def per_domain(item):
        ext, pairs, count = item
        zero = jnp.zeros((blocks + 4 * width, 6, 128), jnp.float32)
        return near_loop(ext, pairs, 0, count, zero)
    acc = lax.map(per_domain, (extended, pair_list, pair_count))
    gforce = acc[:, blocks:].reshape(N_GX, N_GY, 4, width, 6, 128)
    back = jnp.stack([shifted(gforce[:, :, 1], 0, 1), shifted(gforce[:, :, 0], 0, -1), shifted(gforce[:, :, 3], 1, 1), shifted(gforce[:, :, 2], 1, -1)], 2)
    back = back.reshape(domains, 4, width, 6, 128) * slot_ok[..., None, None]
    local = acc[:, :blocks].at[rows, send_blocks].add(back)
    near = local.transpose(2, 0, 1, 3).reshape(6, SEGS)
    moments = jax.ops.segment_sum(moment_terms(ends, burgers).T, seg_cell, num_segments=CELLS).T
    far = far_field(ends, burgers, seg_cell, moments)
    return near + jnp.concatenate([0.5 * far, 0.5 * far], 0)
```

```python
import functools

import jax
import jax.numpy as jnp
from jax import lax
from jax.experimental import pallas as pl
from jax.experimental.pallas import tpu as pltpu
from jax.sharding import PartitionSpec as P

CELL_XY = 8
CELL_Z = 4
CELLS = 256
LANES = 128
TERM_ROWS = 16
CHUNK = 1024

CORE_SQ = 2.5e-05
NEAR_COEF = 0.2
FAR_COEF = 0.2
F32 = jnp.float32
BF16 = jnp.bfloat16
MESH = pl.DeviceIdType.MESH
VMEM_SPEC = pl.BlockSpec(memory_space=pltpu.VMEM)
SMEM_SPEC = pl.BlockSpec(memory_space=pltpu.SMEM)
VMEM_LIMIT = 48 * 1024 * 1024


def split(value):
    high = value.astype(BF16)
    return high, (value - high.astype(F32)).astype(BF16)


def matmul(a, b):
    return jnp.dot(a, b, preferred_element_type=F32)


def at_block(index, rows=8):
    return pl.ds(pl.multiple_of(index * rows, rows), rows)


def at_lanes(index, lanes=LANES):
    return pl.ds(pl.multiple_of(index * lanes, lanes), lanes)


def prepare(width, slots, counts, ends, burgers, cell, main, bz, terms, outgoing, moments):
    blocks = main.shape[0] // 8

    def rows(b, _):
        at = at_lanes(b)
        first, second, burg = ends[0:3, at], ends[3:6, at], burgers[:, at]
        line = second - first
        base = pl.multiple_of(b * 8, 8)
        main[pl.ds(base, 3), :] = 0.5 * (first + second)
        main[pl.ds(base + 3, 3), :] = line
        main[pl.ds(base + 6, 2), :] = burg[0:2]
        bz[pl.ds(b, 1), :] = burg[2:3]
        for p in range(3):
            terms[3 * p : 3 * p + 3, at] = burg[p : p + 1] * line
        terms[9:12, at] = line
        terms[12:16, at] = jnp.zeros((4, LANES), F32)
        return 0

    lax.fori_loop(0, blocks, rows, 0, unroll=4)

    for r in range(4):

        def gather(g, _):
            block = slots[r * width + g]
            keep = jnp.where(g < counts[r], 1.0, 0.0).astype(F32)
            outgoing[r, at_block(g), :] = main[at_block(block), :] * keep
            outgoing[r, pl.ds(8 * width + g, 1), :] = bz[pl.ds(block, 1), :] * keep
            return 0

        lax.fori_loop(0, width, gather, 0, unroll=4)

    per = CHUNK // LANES
    ids = lax.broadcasted_iota(jnp.int32, (CELLS, LANES), 0)

    def add(c, total):
        at = at_lanes(c, CHUNK)
        high, low = split(terms[:, at])
        both = jnp.concatenate([high, low], 0)
        hot = jnp.concatenate(
            [jnp.where(cell[pl.ds(c * per + k, 1), :] == ids, 1.0, 0.0).astype(BF16) for k in range(per)], 1
        )
        return total + lax.dot_general(both, hot, (((1,), (1,)), ((), ())), preferred_element_type=F32)

    total = lax.fori_loop(0, blocks // per, add, jnp.zeros((2 * TERM_ROWS, CELLS), F32))
    moments[...] = total[:TERM_ROWS] + total[TERM_ROWS:]


def hello(sizes):
    barrier = pltpu.get_barrier_semaphore()
    for axis, size in sizes:
        me = lax.axis_index(axis)
        for step in range(1, size):
            pl.semaphore_signal(
                barrier, inc=1, device_id={axis: lax.rem(me + step, size)}, device_id_type=MESH
            )
    pl.semaphore_wait(barrier, sum(size - 1 for _, size in sizes))


def hello_near(sizes):
    barrier = pltpu.get_barrier_semaphore()
    peers = 0
    for axis, size in sizes:
        me = lax.axis_index(axis)
        peers = peers + jnp.where(me > 0, 1, 0) + jnp.where(me < size - 1, 1, 0)
        for step in (-1, 1):
            there = me > 0 if step < 0 else me < size - 1

            @pl.when(there)
            def _():
                pl.semaphore_signal(barrier, inc=1, device_id={axis: me + step}, device_id_type=MESH)

    pl.semaphore_wait(barrier, peers)


def neighbours(sizes, source, target, send_sem, recv_sem):
    out = []
    for r in range(4):
        axis, size = sizes[r // 2]
        me = lax.axis_index(axis)
        step = 1 if r % 2 else -1
        there = me < size - 1 if r % 2 else me > 0
        peer = jnp.clip(me + step, 0, size - 1)
        copy = pltpu.make_async_remote_copy(
            src_ref=source.at[r],
            dst_ref=target.at[r ^ 1],
            send_sem=send_sem.at[r],
            recv_sem=recv_sem.at[r ^ 1],
            device_id={axis: peer},
            device_id_type=MESH,
        )
        back = pltpu.make_async_remote_copy(
            src_ref=source.at[r],
            dst_ref=target.at[r],
            send_sem=send_sem.at[r],
            recv_sem=recv_sem.at[r],
            device_id={axis: peer},
            device_id_type=MESH,
        )
        out.append((there, copy, back))
    return out


def start_all(copies, target):
    for r, (there, copy, _) in enumerate(copies):

        @pl.when(there)
        def _():
            copy.start()

        @pl.when(jnp.logical_not(there))
        def _():
            target[r] = jnp.zeros(target.shape[1:], F32)


def wait_all(copies):
    for there, copy, back in copies:

        @pl.when(there)
        def _():
            copy.wait_send()
            back.wait_recv()


def exchange(sizes, outgoing, local, ghosts, moments, held_x, held_y, partial, send_sem, recv_sem, sx, rx, sy, ry):
    hello(sizes)
    (ax, nx), (ay, ny) = sizes

    def spread(source, axis, size, held, send, recv):
        me = lax.axis_index(axis)
        copies = []
        for step in range(1, size):
            copy = pltpu.make_async_remote_copy(
                src_ref=source,
                dst_ref=held.at[step - 1],
                send_sem=send.at[step - 1],
                recv_sem=recv.at[step - 1],
                device_id={axis: lax.rem(me + step, size)},
                device_id_type=MESH,
            )
            copy.start()
            copies.append(copy)
        return copies

    first = spread(local, ay, ny, held_y, sy, ry)
    copies = neighbours(sizes, outgoing, ghosts, send_sem, recv_sem)
    start_all(copies, ghosts)
    total = local[...]
    for k, copy in enumerate(first):
        copy.wait()
        total = total + held_y[k]
    partial[...] = total
    second = spread(partial, ax, nx, held_x, sx, rx)
    for k, copy in enumerate(second):
        copy.wait()
        total = total + held_x[k]
    moments[...] = total
    wait_all(copies)


def give_back(sizes, forces, returned, send_sem, recv_sem):
    hello_near(sizes)
    copies = neighbours(sizes, forces, returned, send_sem, recv_sem)
    start_all(copies, returned)
    wait_all(copies)


def interact(width, pairs, count, main, bz, ghosts, cell, terms, moments, own_acc, ghost_acc, ext, sym, acc):
    blocks = main.shape[0] // 8
    total = blocks + 4 * width
    acc[...] = jnp.zeros_like(acc)
    ext[0 : 8 * blocks] = main[...]
    for r in range(4):
        lo = 8 * (blocks + r * width)
        ext[lo : lo + 8 * width] = ghosts[r, 0 : 8 * width]

    def products(tile, base, burg_z):
        lx, ly, lz, bx, by = (tile[k : k + 1] for k in (3, 4, 5, 6, 7))
        sym[pl.ds(base, 1), :] = 2.0 * bx * lx
        sym[pl.ds(base + 1, 1), :] = 2.0 * by * ly
        sym[pl.ds(base + 2, 1), :] = 2.0 * burg_z * lz
        sym[pl.ds(base + 3, 1), :] = bx * ly + by * lx
        sym[pl.ds(base + 4, 1), :] = bx * lz + burg_z * lx
        sym[pl.ds(base + 5, 1), :] = by * lz + burg_z * ly
        sym[pl.ds(base + 6, 1), :] = lx * lx + ly * ly + lz * lz
        sym[pl.ds(base + 7, 1), :] = jnp.zeros((1, LANES), F32)

    def own_products(b, _):
        products(main[at_block(b), :], pl.multiple_of(b * 8, 8), bz[pl.ds(b, 1), :])
        return 0

    lax.fori_loop(0, blocks, own_products, 0, unroll=4)
    for r in range(4):

        def ghost_products(g, _):
            base = pl.multiple_of((blocks + r * width + g) * 8, 8)
            products(ghosts[r, at_block(g), :], base, ghosts[r, pl.ds(8 * width + g, 1), :])
            return 0

        lax.fori_loop(0, width, ghost_products, 0, unroll=4)

    sub = lax.broadcasted_iota(jnp.int32, (8, LANES), 0)
    lane = lax.broadcasted_iota(jnp.int32, (8, LANES), 1)
    ahead = lane - sub
    scale = jnp.where(sub < 3, 0.5 * NEAR_COEF, jnp.where(sub < 6, NEAR_COEF, 0.0)).astype(F32)
    empty = jnp.zeros((8, LANES), F32)

    def pair(p, _):
        left = pairs[2 * p]
        right = pairs[2 * p + 1]
        floor = jnp.where(left == right, 0, -1024)
        source = jnp.concatenate([ext[at_block(left), :], sym[at_block(left), :]], 0)
        cols = source.T
        tile_t = ext[at_block(right), :]
        sym_t = sym[at_block(right), :]
        a_high, a_low = split(cols)
        b_high, b_low = split(jnp.concatenate([empty, sym_t * scale], 0))
        dots = matmul(a_high, b_high) + (matmul(a_high, b_low) + matmul(a_low, b_high))
        mt = [jnp.broadcast_to(tile_t[k : k + 1], (8, LANES)) for k in range(3)]
        lt = [jnp.broadcast_to(tile_t[k + 3 : k + 4], (8, LANES)) for k in range(3)]
        len_t = jnp.broadcast_to(sym_t[6:7], (8, LANES))
        sums_t = [empty] * 6
        columns = []
        for c in range(LANES // 8):
            col = cols[8 * c : 8 * c + 8]
            ms = [col[:, k : k + 1] for k in range(3)]
            ls = [col[:, k + 3 : k + 4] for k in range(3)]
            len_s = col[:, 14:15]
            rel = [mt[k] - ms[k] for k in range(3)]
            quad = rel[0] * rel[0] + rel[1] * rel[1] + rel[2] * rel[2] + CORE_SQ
            inv = lax.rsqrt(quad)
            coef = dots[8 * c : 8 * c + 8] * (inv * inv * inv)
            coef = jnp.where(ahead > floor + 8 * c, coef, 0.0)
            push = [coef * rel[k] for k in range(3)]
            along_s = ls[0] * rel[0] + ls[1] * rel[1] + ls[2] * rel[2]
            along_t = lt[0] * rel[0] + lt[1] * rel[1] + lt[2] * rel[2]
            den_s = quad + len_s
            den_t = quad + len_t
            both = den_s * den_t
            near = pl.reciprocal(both, approx=True)
            near = near * (2.0 - both * near)
            half = 0.5 * near
            share_s = along_s * den_t * half
            share_t = along_t * den_s * half
            skew_s = [share_s * push[k] for k in range(3)]
            for k in range(3):
                sums_t[k] = sums_t[k] + push[k]
                sums_t[k + 3] = sums_t[k + 3] - share_t * push[k]
            made = empty
            for k, value in enumerate(push + skew_s):
                made = jnp.where(lane == k, jnp.sum(value, 1, keepdims=True), made)
            columns.append(made)
        rows_s = jnp.concatenate(columns, 0).T[0:8]
        acc[at_block(left), :] = acc[at_block(left), :] - rows_s
        rows_t = empty
        for k in range(6):
            rows_t = jnp.where(sub == k, jnp.sum(sums_t[k], 0, keepdims=True), rows_t)
        acc[at_block(right), :] = acc[at_block(right), :] + rows_t
        return 0

    lax.fori_loop(0, count[0], pair, 0)

    per_x = CELL_XY * CELL_Z
    groups = per_x // 8
    kz = sub % CELL_Z
    kys = [sub // CELL_Z + (8 // CELL_Z) * j for j in range(groups)]
    z_centre = (kz.astype(F32) + 0.5) / (16 * CELL_Z)
    y_centres = [(ky.astype(F32) + 0.5) / CELL_XY for ky in kys]
    m_high, m_low = split(moments[...].T)

    def far(b, _):
        t_high, t_low = split(terms[:, at_lanes(b)])
        weight = matmul(m_high, t_high) + (matmul(m_high, t_low) + matmul(m_low, t_high))
        tile = main[at_block(b), :]
        mx, my, mz = (jnp.broadcast_to(tile[k : k + 1], (8, LANES)) for k in range(3))
        here = jnp.broadcast_to(cell[pl.ds(b, 1), :], (8, LANES))
        cx, cy, cz = here // per_x, here // CELL_Z % CELL_XY, here % CELL_Z
        rz = z_centre - mz
        rys = [centre - my for centre in y_centres]
        flat = [ry * ry + rz * rz + CORE_SQ for ry in rys]
        gap_z = jnp.abs(kz - cz)
        gaps = [jnp.maximum(jnp.abs(ky - cy), gap_z) for ky in kys]
        sums = [empty] * groups
        fx = empty
        for kx in range(CELL_XY):
            rx = (kx + 0.5) / CELL_XY - mx
            square = rx * rx
            gap_x = jnp.abs(cx - kx)
            plane = empty
            for j in range(groups):
                inv = lax.rsqrt(square + flat[j])
                lo = kx * per_x + 8 * j
                coef = weight[lo : lo + 8] * (inv * inv * inv)
                coef = jnp.where(jnp.maximum(gap_x, gaps[j]) >= 2, coef, 0.0)
                sums[j] = sums[j] + coef
                plane = plane + coef
            fx = fx + rx * plane
        fy, fall = empty, empty
        for j in range(groups):
            fy = fy + rys[j] * sums[j]
            fall = fall + sums[j]
        rows = empty
        for k, value in enumerate((fx, fy, rz * fall)):
            rows = jnp.where(sub == k, jnp.sum(value, 0, keepdims=True), rows)
        own_acc[at_block(b), :] = acc[at_block(b), :] + FAR_COEF * rows
        return 0

    lax.fori_loop(0, blocks, far, 0)
    for r in range(4):
        lo = 8 * (blocks + r * width)
        ghost_acc[r] = acc[lo : lo + 8 * width]


def finish(width, slots, counts, own_acc, returned, out, acc):
    blocks = own_acc.shape[0] // 8
    acc[...] = own_acc[...]
    for r in range(4):

        def add(g, _):
            at = at_block(slots[r * width + g])
            acc[at, :] = acc[at, :] + returned[r, at_block(g), :]
            return 0

        lax.fori_loop(0, counts[r], add, 0)

    def write(b, _):
        tile = acc[at_block(b), :]
        both = 0.5 * tile[0:3]
        out[0:3, at_lanes(b)] = both - tile[3:6]
        out[3:6, at_lanes(b)] = both + tile[3:6]
        return 0

    lax.fori_loop(0, blocks, write, 0, unroll=4)


def shape(*dims):
    return jax.ShapeDtypeStruct(dims, F32)


def on_device(sizes, ends, burgers, seg_cell, send_blocks, send_count, pair_list, pair_count):
    seg_here = ends.shape[1]
    blocks = seg_here // LANES
    width = send_blocks.shape[2]
    sent_rows = 9 * width
    (ax, nx), (ay, ny) = sizes
    slots = send_blocks.reshape(-1)
    counts = send_count.reshape(-1)
    cell = seg_cell.reshape(blocks, LANES)
    here = lax.axis_index(ax) * ny + lax.axis_index(ay)
    count = lax.dynamic_slice(pair_count, (here,), (1,))
    params = pltpu.CompilerParams(vmem_limit_bytes=VMEM_LIMIT)

    main, bz, terms, outgoing, local = pl.pallas_call(
        functools.partial(prepare, width),
        out_shape=(
            shape(blocks * 8, LANES),
            shape(blocks, LANES),
            shape(TERM_ROWS, seg_here),
            shape(4, sent_rows, LANES),
            shape(TERM_ROWS, CELLS),
        ),
        in_specs=[SMEM_SPEC] * 2 + [VMEM_SPEC] * 3,
        out_specs=(VMEM_SPEC,) * 5,
        compiler_params=params,
        name="prepare",
    )(slots, counts, ends, burgers, cell)

    dma = pltpu.SemaphoreType.DMA
    ghosts, moments = pl.pallas_call(
        functools.partial(exchange, sizes),
        out_shape=(shape(4, sent_rows, LANES), shape(TERM_ROWS, CELLS)),
        in_specs=[VMEM_SPEC] * 2,
        out_specs=(VMEM_SPEC,) * 2,
        scratch_shapes=[
            pltpu.VMEM((nx - 1, TERM_ROWS, CELLS), F32),
            pltpu.VMEM((ny - 1, TERM_ROWS, CELLS), F32),
            pltpu.VMEM((TERM_ROWS, CELLS), F32),
            dma((4,)),
            dma((4,)),
            dma((nx - 1,)),
            dma((nx - 1,)),
            dma((ny - 1,)),
            dma((ny - 1,)),
        ],
        compiler_params=pltpu.CompilerParams(
            collective_id=0, has_side_effects=True, vmem_limit_bytes=VMEM_LIMIT
        ),
        name="exchange",
    )(outgoing, local)

    own_acc, ghost_acc = pl.pallas_call(
        functools.partial(interact, width),
        out_shape=(shape(blocks * 8, LANES), shape(4, 8 * width, LANES)),
        in_specs=[SMEM_SPEC] * 2 + [VMEM_SPEC] * 6,
        out_specs=(VMEM_SPEC,) * 2,
        scratch_shapes=[pltpu.VMEM(((blocks + 4 * width) * 8, LANES), F32)] * 3,
        compiler_params=params,
        name="interact",
    )(pair_list.reshape(-1), count, main, bz, ghosts, cell, terms, moments)

    returned = pl.pallas_call(
        functools.partial(give_back, sizes),
        out_shape=shape(4, 8 * width, LANES),
        in_specs=[VMEM_SPEC],
        out_specs=VMEM_SPEC,
        scratch_shapes=[dma((4,)), dma((4,))],
        compiler_params=pltpu.CompilerParams(
            collective_id=1, has_side_effects=True, vmem_limit_bytes=VMEM_LIMIT
        ),
        name="give_back",
    )(ghost_acc)

    return pl.pallas_call(
        functools.partial(finish, width),
        out_shape=shape(6, seg_here),
        in_specs=[SMEM_SPEC] * 2 + [VMEM_SPEC] * 2,
        out_specs=VMEM_SPEC,
        scratch_shapes=[pltpu.VMEM((blocks * 8, LANES), F32)],
        compiler_params=params,
        name="finish",
    )(slots, counts, own_acc, returned)


def solution(mesh):
    sizes = (("gx", mesh.shape["gx"]), ("gy", mesh.shape["gy"]))
    return jax.shard_map(
        functools.partial(on_device, sizes),
        mesh=mesh,
        in_specs=(
            P(None, ("gx", "gy")),
            P(None, ("gx", "gy")),
            P(("gx", "gy")),
            P(("gx", "gy"), None, None),
            P(("gx", "gy"), None),
            P(("gx", "gy"), None, None),
            P(),
        ),
        out_specs=P(None, ("gx", "gy")),
        check_vma=False,
    )
```

```python
import functools

import jax
import jax.numpy as jnp
from jax import lax
from jax.experimental import pallas as pl
from jax.experimental.pallas import tpu as pltpu
from jax.sharding import PartitionSpec as P

CELL_XY = 8
CELL_Z = 4
CELLS = 256
LANES = 128
TERM_ROWS = 16
CHUNK = 1024

CORE_SQ = 2.5e-05
NEAR_COEF = 0.2
FAR_COEF = 0.2
F32 = jnp.float32
BF16 = jnp.bfloat16
MESH = pl.DeviceIdType.MESH
VMEM_SPEC = pl.BlockSpec(memory_space=pltpu.VMEM)
SMEM_SPEC = pl.BlockSpec(memory_space=pltpu.SMEM)
VMEM_LIMIT = 48 * 1024 * 1024


def split(value):
    high = value.astype(BF16)
    return high, (value - high.astype(F32)).astype(BF16)


def matmul(a, b):
    return jnp.dot(a, b, preferred_element_type=F32)


def at_block(index, rows=8):
    return pl.ds(pl.multiple_of(index * rows, rows), rows)


def at_lanes(index, lanes=LANES):
    return pl.ds(pl.multiple_of(index * lanes, lanes), lanes)


def prepare(width, slots, counts, ends, burgers, cell, main, bz, terms, outgoing, moments):
    blocks = main.shape[0] // 8

    def rows(b, _):
        at = at_lanes(b)
        first, second, burg = ends[0:3, at], ends[3:6, at], burgers[:, at]
        line = second - first
        base = pl.multiple_of(b * 8, 8)
        main[pl.ds(base, 3), :] = 0.5 * (first + second)
        main[pl.ds(base + 3, 3), :] = line
        main[pl.ds(base + 6, 2), :] = burg[0:2]
        bz[pl.ds(b, 1), :] = burg[2:3]
        for p in range(3):
            terms[3 * p : 3 * p + 3, at] = burg[p : p + 1] * line
        terms[9:12, at] = line
        terms[12:16, at] = jnp.zeros((4, LANES), F32)
        return 0

    lax.fori_loop(0, blocks, rows, 0, unroll=4)

    for r in range(4):

        def gather(g, _):
            block = slots[r * width + g]
            keep = jnp.where(g < counts[r], 1.0, 0.0).astype(F32)
            outgoing[r, at_block(g), :] = main[at_block(block), :] * keep
            outgoing[r, pl.ds(8 * width + g, 1), :] = bz[pl.ds(block, 1), :] * keep
            return 0

        lax.fori_loop(0, width, gather, 0, unroll=4)

    per = CHUNK // LANES
    ids = lax.broadcasted_iota(jnp.int32, (CELLS, LANES), 0)

    def add(c, total):
        at = at_lanes(c, CHUNK)
        high, low = split(terms[:, at])
        both = jnp.concatenate([high, low], 0)
        hot = jnp.concatenate(
            [jnp.where(cell[pl.ds(c * per + k, 1), :] == ids, 1.0, 0.0).astype(BF16) for k in range(per)], 1
        )
        return total + lax.dot_general(both, hot, (((1,), (1,)), ((), ())), preferred_element_type=F32)

    total = lax.fori_loop(0, blocks // per, add, jnp.zeros((2 * TERM_ROWS, CELLS), F32))
    moments[...] = total[:TERM_ROWS] + total[TERM_ROWS:]


def hello(sizes):
    barrier = pltpu.get_barrier_semaphore()
    for axis, size in sizes:
        me = lax.axis_index(axis)
        for step in range(1, size):
            pl.semaphore_signal(
                barrier, inc=1, device_id={axis: lax.rem(me + step, size)}, device_id_type=MESH
            )
    pl.semaphore_wait(barrier, sum(size - 1 for _, size in sizes))


def hello_near(sizes):
    barrier = pltpu.get_barrier_semaphore()
    peers = 0
    for axis, size in sizes:
        me = lax.axis_index(axis)
        peers = peers + jnp.where(me > 0, 1, 0) + jnp.where(me < size - 1, 1, 0)
        for step in (-1, 1):
            there = me > 0 if step < 0 else me < size - 1

            @pl.when(there)
            def _():
                pl.semaphore_signal(barrier, inc=1, device_id={axis: me + step}, device_id_type=MESH)

    pl.semaphore_wait(barrier, peers)


def neighbours(sizes, source, target, send_sem, recv_sem):
    out = []
    for r in range(4):
        axis, size = sizes[r // 2]
        me = lax.axis_index(axis)
        step = 1 if r % 2 else -1
        there = me < size - 1 if r % 2 else me > 0
        peer = jnp.clip(me + step, 0, size - 1)
        copy = pltpu.make_async_remote_copy(
            src_ref=source.at[r],
            dst_ref=target.at[r ^ 1],
            send_sem=send_sem.at[r],
            recv_sem=recv_sem.at[r ^ 1],
            device_id={axis: peer},
            device_id_type=MESH,
        )
        back = pltpu.make_async_remote_copy(
            src_ref=source.at[r],
            dst_ref=target.at[r],
            send_sem=send_sem.at[r],
            recv_sem=recv_sem.at[r],
            device_id={axis: peer},
            device_id_type=MESH,
        )
        out.append((there, copy, back))
    return out


def start_all(copies, target):
    for r, (there, copy, _) in enumerate(copies):

        @pl.when(there)
        def _():
            copy.start()

        @pl.when(jnp.logical_not(there))
        def _():
            target[r] = jnp.zeros(target.shape[1:], F32)


def wait_all(copies):
    for there, copy, back in copies:

        @pl.when(there)
        def _():
            copy.wait_send()
            back.wait_recv()


def exchange(sizes, outgoing, local, ghosts, moments, held_x, held_y, partial, send_sem, recv_sem, sx, rx, sy, ry):
    hello(sizes)
    (ax, nx), (ay, ny) = sizes

    def spread(source, axis, size, held, send, recv):
        me = lax.axis_index(axis)
        copies = []
        for step in range(1, size):
            copy = pltpu.make_async_remote_copy(
                src_ref=source,
                dst_ref=held.at[step - 1],
                send_sem=send.at[step - 1],
                recv_sem=recv.at[step - 1],
                device_id={axis: lax.rem(me + step, size)},
                device_id_type=MESH,
            )
            copy.start()
            copies.append(copy)
        return copies

    first = spread(local, ay, ny, held_y, sy, ry)
    copies = neighbours(sizes, outgoing, ghosts, send_sem, recv_sem)
    start_all(copies, ghosts)
    total = local[...]
    for k, copy in enumerate(first):
        copy.wait()
        total = total + held_y[k]
    partial[...] = total
    second = spread(partial, ax, nx, held_x, sx, rx)
    for k, copy in enumerate(second):
        copy.wait()
        total = total + held_x[k]
    moments[...] = total
    wait_all(copies)


def give_back(sizes, forces, returned, send_sem, recv_sem):
    hello_near(sizes)
    copies = neighbours(sizes, forces, returned, send_sem, recv_sem)
    start_all(copies, returned)
    wait_all(copies)


def interact(
    width, pairs, count, main, bz, ghosts, cell, terms, moments, own_acc, ghost_acc, ext, sym, acc, cols, dots, made
):
    blocks = main.shape[0] // 8
    total = blocks + 4 * width
    acc[...] = jnp.zeros_like(acc)
    ext[0 : 8 * blocks] = main[...]
    for r in range(4):
        lo = 8 * (blocks + r * width)
        ext[lo : lo + 8 * width] = ghosts[r, 0 : 8 * width]

    def products(first, many, burg_z):
        def row(k):
            return pl.ds(8 * first + k, many, stride=8)

        lx, ly, lz, bx, by = (ext[row(k), :] for k in (3, 4, 5, 6, 7))
        sym[row(0), :] = 2.0 * bx * lx
        sym[row(1), :] = 2.0 * by * ly
        sym[row(2), :] = 2.0 * burg_z * lz
        sym[row(3), :] = bx * ly + by * lx
        sym[row(4), :] = bx * lz + burg_z * lx
        sym[row(5), :] = by * lz + burg_z * ly
        zero = jnp.zeros((many, LANES), F32)
        sym[row(6), :] = zero
        sym[row(7), :] = zero
        ext[row(6), :] = lx * lx + ly * ly + lz * lz

    for b in range(0, blocks, 8):
        products(b, 8, bz[b : b + 8])
    for r in range(4):
        for g in range(0, width, 8):
            products(blocks + r * width + g, 8, ghosts[r, 8 * width + g : 8 * width + g + 8])

    sub = lax.broadcasted_iota(jnp.int32, (8, LANES), 0)
    lane = lax.broadcasted_iota(jnp.int32, (8, LANES), 1)
    ahead = lane - sub
    scale = jnp.where(sub < 3, 0.5 * NEAR_COEF, jnp.where(sub < 6, NEAR_COEF, 0.0)).astype(F32)
    empty = jnp.zeros((8, LANES), F32)
    listed = count[0]

    def loop(body, at_once):
        def several(q, _):
            body([q * at_once + k for k in range(at_once)])
            return 0

        lax.fori_loop(0, (listed + 3) // 4 * (4 // at_once), several, 0)

    def halves(value):
        high, low = split(value)
        return high.astype(F32), low.astype(F32)

    def turn(group):
        for p in group:
            left, right = pairs[2 * p], pairs[2 * p + 1]
            s_high, s_low = halves(sym[at_block(left), :])
            t_high, t_low = halves(sym[at_block(right), :] * scale)
            col = jnp.concatenate([ext[at_block(left), :], s_high, s_high, s_low], 0).T
            other = jnp.concatenate([empty, t_high, t_low, t_high], 0)
            cols[p, :, 0:32] = col
            dots[p] = matmul(col.astype(BF16), other.astype(BF16))

    def forces(group):
        for p in group:
            left, right = pairs[2 * p], pairs[2 * p + 1]
            floor = jnp.where(left == right, 0, -1024)
            floor = jnp.where(p < listed, floor, 1024)
            tile_t = ext[at_block(right), :]
            mt = [jnp.broadcast_to(tile_t[k : k + 1], (8, LANES)) for k in range(3)]
            lt = [jnp.broadcast_to(tile_t[k + 3 : k + 4], (8, LANES)) for k in range(3)]
            len_t = jnp.broadcast_to(tile_t[6:7], (8, LANES))
            sums_t = [empty] * 6
            for c in range(LANES // 8):
                col = cols[p, 8 * c : 8 * c + 8, :]
                ms = [col[:, k : k + 1] for k in range(3)]
                ls = [col[:, k + 3 : k + 4] for k in range(3)]
                len_s = col[:, 6:7]
                rel = [mt[k] - ms[k] for k in range(3)]
                quad = rel[0] * rel[0] + rel[1] * rel[1] + rel[2] * rel[2] + CORE_SQ
                inv = lax.rsqrt(quad)
                coef = dots[p, 8 * c : 8 * c + 8, :] * (inv * inv * inv)
                coef = jnp.where(ahead > floor + 8 * c, coef, 0.0)
                push = [coef * rel[k] for k in range(3)]
                along_s = ls[0] * rel[0] + ls[1] * rel[1] + ls[2] * rel[2]
                along_t = lt[0] * rel[0] + lt[1] * rel[1] + lt[2] * rel[2]
                den_s = quad + len_s
                den_t = quad + len_t
                both = den_s * den_t
                near = pl.reciprocal(both, approx=True)
                near = near * (2.0 - both * near)
                half = 0.5 * near
                share_s = along_s * den_t * half
                share_t = along_t * den_s * half
                skew_s = [share_s * push[k] for k in range(3)]
                for k in range(3):
                    sums_t[k] = sums_t[k] + push[k]
                    sums_t[k + 3] = sums_t[k + 3] - share_t * push[k]
                wide = empty
                for k, value in enumerate(push + skew_s):
                    wide = jnp.where(lane == k, jnp.sum(value, 1, keepdims=True), wide)
                made[p, 8 * c : 8 * c + 8, :] = wide
            rows_t = empty
            for k in range(6):
                rows_t = jnp.where(sub == k, jnp.sum(sums_t[k], 0, keepdims=True), rows_t)
            made[p, LANES : LANES + 8, :] = rows_t

    def collect(group):
        rows_s = [made[p, 0:LANES, :].T[0:8] for p in group]
        rows_t = [made[p, LANES : LANES + 8, :] for p in group]
        for k, p in enumerate(group):
            left, right = pairs[2 * p], pairs[2 * p + 1]
            acc[at_block(left), :] = acc[at_block(left), :] - rows_s[k]
            acc[at_block(right), :] = acc[at_block(right), :] + rows_t[k]

    loop(turn, 4)
    loop(forces, 2)
    loop(collect, 4)

    per_x = CELL_XY * CELL_Z
    groups = per_x // 8
    kz = sub % CELL_Z
    kys = [sub // CELL_Z + (8 // CELL_Z) * j for j in range(groups)]
    z_centre = (kz.astype(F32) + 0.5) / (16 * CELL_Z)
    y_centres = [(ky.astype(F32) + 0.5) / CELL_XY for ky in kys]
    m_high, m_low = split(moments[...])
    m_cols = jnp.concatenate([m_high.astype(F32), m_high.astype(F32), m_low.astype(F32)], 0).T.astype(BF16)

    def far(b, _):
        t_high, t_low = split(terms[:, at_lanes(b)])
        weight = matmul(m_cols, jnp.concatenate([t_high, t_low, t_high], 0))
        tile = main[at_block(b), :]
        mx, my, mz = (jnp.broadcast_to(tile[k : k + 1], (8, LANES)) for k in range(3))
        here = jnp.broadcast_to(cell[pl.ds(b, 1), :], (8, LANES))
        cx, cy, cz = here // per_x, here // CELL_Z % CELL_XY, here % CELL_Z
        rz = z_centre - mz
        rys = [centre - my for centre in y_centres]
        flat = [ry * ry + rz * rz + CORE_SQ for ry in rys]
        gap_z = jnp.abs(kz - cz)
        gaps = [jnp.maximum(jnp.abs(ky - cy), gap_z) for ky in kys]
        sums = [empty] * groups
        fx = empty
        for kx in range(CELL_XY):
            rx = (kx + 0.5) / CELL_XY - mx
            square = rx * rx
            gap_x = jnp.abs(cx - kx)
            plane = empty
            for j in range(groups):
                inv = lax.rsqrt(square + flat[j])
                lo = kx * per_x + 8 * j
                coef = weight[lo : lo + 8] * (inv * inv * inv)
                coef = jnp.where(jnp.maximum(gap_x, gaps[j]) >= 2, coef, 0.0)
                sums[j] = sums[j] + coef
                plane = plane + coef
            fx = fx + rx * plane
        fy, fall = empty, empty
        for j in range(groups):
            fy = fy + rys[j] * sums[j]
            fall = fall + sums[j]
        rows = empty
        for k, value in enumerate((fx, fy, rz * fall)):
            rows = jnp.where(sub == k, jnp.sum(value, 0, keepdims=True), rows)
        own_acc[at_block(b), :] = acc[at_block(b), :] + FAR_COEF * rows
        return 0

    lax.fori_loop(0, blocks, far, 0, unroll=4)
    for r in range(4):
        lo = 8 * (blocks + r * width)
        ghost_acc[r] = acc[lo : lo + 8 * width]


def finish(width, slots, counts, own_acc, returned, out, acc):
    blocks = own_acc.shape[0] // 8
    acc[...] = own_acc[...]
    for r in range(4):

        def add(g, _):
            at = at_block(slots[r * width + g])
            acc[at, :] = acc[at, :] + returned[r, at_block(g), :]
            return 0

        lax.fori_loop(0, counts[r], add, 0)

    def write(b, _):
        tile = acc[at_block(b), :]
        both = 0.5 * tile[0:3]
        out[0:3, at_lanes(b)] = both - tile[3:6]
        out[3:6, at_lanes(b)] = both + tile[3:6]
        return 0

    lax.fori_loop(0, blocks, write, 0, unroll=4)


def shape(*dims):
    return jax.ShapeDtypeStruct(dims, F32)


def on_device(sizes, ends, burgers, seg_cell, send_blocks, send_count, pair_list, pair_count):
    seg_here = ends.shape[1]
    blocks = seg_here // LANES
    width = send_blocks.shape[2]
    sent_rows = 9 * width
    most = pair_list.shape[1]
    (ax, nx), (ay, ny) = sizes
    slots = send_blocks.reshape(-1)
    counts = send_count.reshape(-1)
    cell = seg_cell.reshape(blocks, LANES)
    here = lax.axis_index(ax) * ny + lax.axis_index(ay)
    count = lax.dynamic_slice(pair_count, (here,), (1,))
    params = pltpu.CompilerParams(vmem_limit_bytes=VMEM_LIMIT)

    main, bz, terms, outgoing, local = pl.pallas_call(
        functools.partial(prepare, width),
        out_shape=(
            shape(blocks * 8, LANES),
            shape(blocks, LANES),
            shape(TERM_ROWS, seg_here),
            shape(4, sent_rows, LANES),
            shape(TERM_ROWS, CELLS),
        ),
        in_specs=[SMEM_SPEC] * 2 + [VMEM_SPEC] * 3,
        out_specs=(VMEM_SPEC,) * 5,
        compiler_params=params,
        name="prepare",
    )(slots, counts, ends, burgers, cell)

    dma = pltpu.SemaphoreType.DMA
    ghosts, moments = pl.pallas_call(
        functools.partial(exchange, sizes),
        out_shape=(shape(4, sent_rows, LANES), shape(TERM_ROWS, CELLS)),
        in_specs=[VMEM_SPEC] * 2,
        out_specs=(VMEM_SPEC,) * 2,
        scratch_shapes=[
            pltpu.VMEM((nx - 1, TERM_ROWS, CELLS), F32),
            pltpu.VMEM((ny - 1, TERM_ROWS, CELLS), F32),
            pltpu.VMEM((TERM_ROWS, CELLS), F32),
            dma((4,)),
            dma((4,)),
            dma((nx - 1,)),
            dma((nx - 1,)),
            dma((ny - 1,)),
            dma((ny - 1,)),
        ],
        compiler_params=pltpu.CompilerParams(
            collective_id=0, has_side_effects=True, vmem_limit_bytes=VMEM_LIMIT
        ),
        name="exchange",
    )(outgoing, local)

    own_acc, ghost_acc = pl.pallas_call(
        functools.partial(interact, width),
        out_shape=(shape(blocks * 8, LANES), shape(4, 8 * width, LANES)),
        in_specs=[SMEM_SPEC] * 2 + [VMEM_SPEC] * 6,
        out_specs=(VMEM_SPEC,) * 2,
        scratch_shapes=[pltpu.VMEM(((blocks + 4 * width) * 8, LANES), F32)] * 3
        + [pltpu.VMEM((most, LANES, LANES), F32)] * 2
        + [pltpu.VMEM((most, LANES + 8, LANES), F32)],
        compiler_params=params,
        name="interact",
    )(pair_list.reshape(-1), count, main, bz, ghosts, cell, terms, moments)

    returned = pl.pallas_call(
        functools.partial(give_back, sizes),
        out_shape=shape(4, 8 * width, LANES),
        in_specs=[VMEM_SPEC],
        out_specs=VMEM_SPEC,
        scratch_shapes=[dma((4,)), dma((4,))],
        compiler_params=pltpu.CompilerParams(
            collective_id=1, has_side_effects=True, vmem_limit_bytes=VMEM_LIMIT
        ),
        name="give_back",
    )(ghost_acc)

    return pl.pallas_call(
        functools.partial(finish, width),
        out_shape=shape(6, seg_here),
        in_specs=[SMEM_SPEC] * 2 + [VMEM_SPEC] * 2,
        out_specs=VMEM_SPEC,
        scratch_shapes=[pltpu.VMEM((blocks * 8, LANES), F32)],
        compiler_params=params,
        name="finish",
    )(slots, counts, own_acc, returned)


def solution(mesh):
    sizes = (("gx", mesh.shape["gx"]), ("gy", mesh.shape["gy"]))
    return jax.shard_map(
        functools.partial(on_device, sizes),
        mesh=mesh,
        in_specs=(
            P(None, ("gx", "gy")),
            P(None, ("gx", "gy")),
            P(("gx", "gy")),
            P(("gx", "gy"), None, None),
            P(("gx", "gy"), None),
            P(("gx", "gy"), None, None),
            P(),
        ),
        out_specs=P(None, ("gx", "gy")),
        check_vma=False,
    )
```

```python
import functools

import jax
import jax.numpy as jnp
from jax import lax
from jax.experimental import pallas as pl
from jax.experimental.pallas import tpu as pltpu
from jax.sharding import PartitionSpec as P

CELL_XY = 8
CELL_Z = 4
CELLS = 256
LANES = 128
TERM_ROWS = 16
CHUNK = 1024
AT_ONCE = 2

CORE_SQ = 2.5e-05
NEAR_COEF = 0.2
FAR_COEF = 0.2
F32 = jnp.float32
BF16 = jnp.bfloat16
MESH = pl.DeviceIdType.MESH
VMEM_SPEC = pl.BlockSpec(memory_space=pltpu.VMEM)
SMEM_SPEC = pl.BlockSpec(memory_space=pltpu.SMEM)
VMEM_LIMIT = 48 * 1024 * 1024


def split(value):
    high = value.astype(BF16)
    return high, (value - high.astype(F32)).astype(BF16)


def matmul(a, b):
    return jnp.dot(a, b, preferred_element_type=F32)


def at_block(index, rows=8):
    return pl.ds(pl.multiple_of(index * rows, rows), rows)


def at_lanes(index, lanes=LANES):
    return pl.ds(pl.multiple_of(index * lanes, lanes), lanes)


def prepare(width, slots, counts, ends, burgers, cell, main, bz, terms, outgoing, moments):
    blocks = main.shape[0] // 8

    def rows(b, _):
        at = at_lanes(b)
        first, second, burg = ends[0:3, at], ends[3:6, at], burgers[:, at]
        line = second - first
        base = pl.multiple_of(b * 8, 8)
        main[pl.ds(base, 3), :] = 0.5 * (first + second)
        main[pl.ds(base + 3, 3), :] = line
        main[pl.ds(base + 6, 2), :] = burg[0:2]
        bz[pl.ds(b, 1), :] = burg[2:3]
        for p in range(3):
            terms[3 * p : 3 * p + 3, at] = burg[p : p + 1] * line
        terms[9:12, at] = line
        terms[12:16, at] = jnp.zeros((4, LANES), F32)
        return 0

    lax.fori_loop(0, blocks, rows, 0, unroll=4)

    for r in range(4):

        def gather(g, _):
            block = slots[r * width + g]
            keep = jnp.where(g < counts[r], 1.0, 0.0).astype(F32)
            outgoing[r, at_block(g), :] = main[at_block(block), :] * keep
            outgoing[r, pl.ds(8 * width + g, 1), :] = bz[pl.ds(block, 1), :] * keep
            return 0

        lax.fori_loop(0, width, gather, 0, unroll=4)

    per = CHUNK // LANES
    ids = lax.broadcasted_iota(jnp.int32, (CELLS, LANES), 0)

    def add(c, total):
        at = at_lanes(c, CHUNK)
        high, low = split(terms[:, at])
        both = jnp.concatenate([high, low], 0)
        hot = jnp.concatenate(
            [jnp.where(cell[pl.ds(c * per + k, 1), :] == ids, 1.0, 0.0).astype(BF16) for k in range(per)], 1
        )
        return total + lax.dot_general(both, hot, (((1,), (1,)), ((), ())), preferred_element_type=F32)

    total = lax.fori_loop(0, blocks // per, add, jnp.zeros((2 * TERM_ROWS, CELLS), F32))
    moments[...] = total[:TERM_ROWS] + total[TERM_ROWS:]


def hello(sizes):
    barrier = pltpu.get_barrier_semaphore()
    for axis, size in sizes:
        me = lax.axis_index(axis)
        for step in range(1, size):
            pl.semaphore_signal(
                barrier, inc=1, device_id={axis: lax.rem(me + step, size)}, device_id_type=MESH
            )
    pl.semaphore_wait(barrier, sum(size - 1 for _, size in sizes))


def hello_near(sizes):
    barrier = pltpu.get_barrier_semaphore()
    peers = 0
    for axis, size in sizes:
        me = lax.axis_index(axis)
        peers = peers + jnp.where(me > 0, 1, 0) + jnp.where(me < size - 1, 1, 0)
        for step in (-1, 1):
            there = me > 0 if step < 0 else me < size - 1

            @pl.when(there)
            def _():
                pl.semaphore_signal(barrier, inc=1, device_id={axis: me + step}, device_id_type=MESH)

    pl.semaphore_wait(barrier, peers)


def neighbours(sizes, source, target, send_sem, recv_sem):
    out = []
    for r in range(4):
        axis, size = sizes[r // 2]
        me = lax.axis_index(axis)
        step = 1 if r % 2 else -1
        there = me < size - 1 if r % 2 else me > 0
        peer = jnp.clip(me + step, 0, size - 1)
        copy = pltpu.make_async_remote_copy(
            src_ref=source.at[r],
            dst_ref=target.at[r ^ 1],
            send_sem=send_sem.at[r],
            recv_sem=recv_sem.at[r ^ 1],
            device_id={axis: peer},
            device_id_type=MESH,
        )
        back = pltpu.make_async_remote_copy(
            src_ref=source.at[r],
            dst_ref=target.at[r],
            send_sem=send_sem.at[r],
            recv_sem=recv_sem.at[r],
            device_id={axis: peer},
            device_id_type=MESH,
        )
        out.append((there, copy, back))
    return out


def start_all(copies, target):
    for r, (there, copy, _) in enumerate(copies):

        @pl.when(there)
        def _():
            copy.start()

        @pl.when(jnp.logical_not(there))
        def _():
            target[r] = jnp.zeros(target.shape[1:], F32)


def wait_all(copies):
    for there, copy, back in copies:

        @pl.when(there)
        def _():
            copy.wait_send()
            back.wait_recv()


def exchange(sizes, outgoing, local, ghosts, moments, held_x, held_y, partial, send_sem, recv_sem, sx, rx, sy, ry):
    hello(sizes)
    (ax, nx), (ay, ny) = sizes

    def spread(source, axis, size, held, send, recv):
        me = lax.axis_index(axis)
        copies = []
        for step in range(1, size):
            copy = pltpu.make_async_remote_copy(
                src_ref=source,
                dst_ref=held.at[step - 1],
                send_sem=send.at[step - 1],
                recv_sem=recv.at[step - 1],
                device_id={axis: lax.rem(me + step, size)},
                device_id_type=MESH,
            )
            copy.start()
            copies.append(copy)
        return copies

    first = spread(local, ay, ny, held_y, sy, ry)
    copies = neighbours(sizes, outgoing, ghosts, send_sem, recv_sem)
    start_all(copies, ghosts)
    total = local[...]
    for k, copy in enumerate(first):
        copy.wait()
        total = total + held_y[k]
    partial[...] = total
    second = spread(partial, ax, nx, held_x, sx, rx)
    for k, copy in enumerate(second):
        copy.wait()
        total = total + held_x[k]
    moments[...] = total
    wait_all(copies)


def give_back(sizes, forces, returned, send_sem, recv_sem):
    hello_near(sizes)
    copies = neighbours(sizes, forces, returned, send_sem, recv_sem)
    start_all(copies, returned)
    wait_all(copies)


def interact(
    width, pairs, count, main, bz, ghosts, cell, terms, moments, own_acc, ghost_acc, ext, sym, acc, rhs, wide, xs
):
    blocks = main.shape[0] // 8
    total = blocks + 4 * width
    acc[...] = jnp.zeros_like(acc)
    ext[0 : 8 * blocks] = main[...]
    for r in range(4):
        lo = 8 * (blocks + r * width)
        ext[lo : lo + 8 * width] = ghosts[r, 0 : 8 * width]

    def products(first, many, burg_z):
        def row(k):
            return pl.ds(8 * first + k, many, stride=8)

        lx, ly, lz, bx, by = (ext[row(k), :] for k in (3, 4, 5, 6, 7))
        sym[row(0), :] = 2.0 * bx * lx
        sym[row(1), :] = 2.0 * by * ly
        sym[row(2), :] = 2.0 * burg_z * lz
        sym[row(3), :] = bx * ly + by * lx
        sym[row(4), :] = bx * lz + burg_z * lx
        sym[row(5), :] = by * lz + burg_z * ly
        zero = jnp.zeros((many, LANES), F32)
        sym[row(6), :] = zero
        sym[row(7), :] = zero
        ext[row(6), :] = lx * lx + ly * ly + lz * lz

    for b in range(0, blocks, 8):
        products(b, 8, bz[b : b + 8])
    for r in range(4):
        for g in range(0, width, 8):
            products(blocks + r * width + g, 8, ghosts[r, 8 * width + g : 8 * width + g + 8])

    sub = lax.broadcasted_iota(jnp.int32, (8, LANES), 0)
    ahead = lax.broadcasted_iota(jnp.int32, (16, LANES), 1) - lax.broadcasted_iota(jnp.int32, (16, LANES), 0)
    scale = jnp.where(sub < 3, 0.5 * NEAR_COEF, jnp.where(sub < 6, NEAR_COEF, 0.0)).astype(F32)
    empty = jnp.zeros((8, LANES), F32)
    listed = count[0]

    def parts(value, many):
        out = []
        for _ in range(many):
            part = value.astype(BF16).astype(F32)
            out.append(part)
            value = value - part
        return out

    depth, across = rhs.shape[1:]
    row = lax.broadcasted_iota(jnp.int32, (depth, across), 0)
    out_id = lax.broadcasted_iota(jnp.int32, (depth, across), 1) // LANES - 1
    pick = jnp.where(out_id < 3, -1.0, 1.0)
    pattern = jnp.where(jnp.logical_and(row < 24, row % 8 == out_id), pick, 0.0).astype(BF16)
    for slot in range(AT_ONCE):
        rhs[slot] = pattern
    ones = jnp.ones((8, LANES), F32)
    edge = [jnp.where(sub == k, -1.0, 0.0).astype(F32) for k in range(3)]
    summed = xs.shape[2]
    adder = jnp.where(
        lax.broadcasted_iota(jnp.int32, (8, summed), 1) // (2 * LANES)
        == lax.broadcasted_iota(jnp.int32, (8, summed), 0),
        1.0,
        0.0,
    ).astype(BF16)

    def turn(slot, p):
        left, right = pairs[2 * p], pairs[2 * p + 1]
        s_high, s_low = parts(sym[at_block(left), :], 2)
        t_high, t_low = parts(sym[at_block(right), :] * scale, 2)
        own = parts(ext[at_block(left), :], 3)
        other = parts(ext[at_block(right), :], 3)
        col = jnp.concatenate(own + [ones] * 3 + [s_high, s_high, s_low, empty], 0).T
        rhs[slot, 48:80, 0:LANES] = jnp.concatenate([t_high, t_low, t_high, empty], 0).astype(BF16)
        for k in range(3):
            keep = jnp.where(sub == k, 1.0, 0.0)
            rows = jnp.concatenate([edge[k]] + [part * keep for part in other], 0)
            rhs[slot, 16:48, (k + 1) * LANES : (k + 2) * LANES] = rows.astype(BF16)
        wide[slot] = matmul(col.astype(BF16), rhs[slot])

    def forces(slot, p):
        left, right = pairs[2 * p], pairs[2 * p + 1]
        floor = jnp.where(left == right, 0, -1024)
        floor = jnp.where(p < listed, floor, 1024)
        tile_t = ext[at_block(right), :]
        lt = [tile_t[k + 3 : k + 4] for k in range(3)]
        len_t = tile_t[6:7]
        sums_t = [jnp.zeros((8, LANES), F32)] * 6
        for c in range(LANES // 16):
            lo = 16 * c
            known = [wide[slot, lo : lo + 16, k * LANES : (k + 1) * LANES] for k in range(8)]
            rel, ls, len_s = known[1:4], known[4:7], known[7]
            quad = rel[0] * rel[0] + rel[1] * rel[1] + rel[2] * rel[2] + CORE_SQ
            inv = lax.rsqrt(quad)
            coef = known[0] * (inv * inv * inv)
            coef = jnp.where(ahead > floor + lo, coef, 0.0)
            push = [coef * rel[k] for k in range(3)]
            along_s = ls[0] * rel[0] + ls[1] * rel[1] + ls[2] * rel[2]
            along_t = lt[0] * rel[0] + lt[1] * rel[1] + lt[2] * rel[2]
            den_s = quad + len_s
            den_t = quad + len_t
            both = den_s * den_t
            near = pl.reciprocal(both, approx=True)
            near = near * (2.0 - both * near)
            half = 0.5 * near
            share_s = along_s * den_t * half
            share_t = along_t * den_s * half
            for k in range(3):
                skew = share_t * push[k]
                sums_t[k] = sums_t[k] + (push[k][0:8] + push[k][8:16])
                sums_t[k + 3] = sums_t[k + 3] - (skew[0:8] + skew[8:16])
            for k, value in enumerate(push + [share_s * push[k] for k in range(3)]):
                high, low = split(value)
                xs[slot, lo : lo + 16, 2 * k * LANES : (2 * k + 1) * LANES] = high
                xs[slot, lo : lo + 16, (2 * k + 1) * LANES : (2 * k + 2) * LANES] = low
        rows_t = empty
        for k in range(6):
            rows_t = jnp.where(sub == k, jnp.sum(sums_t[k], 0, keepdims=True), rows_t)
        rows_s = lax.dot_general(adder, xs[slot], (((1,), (1,)), ((), ())), preferred_element_type=F32)
        return rows_s, rows_t

    def several(q, _):
        group = [(slot, q * AT_ONCE + slot) for slot in range(AT_ONCE)]
        for slot, p in group:
            turn(slot, p)
        rows = [forces(slot, p) for slot, p in group]
        for slot, p in group:
            left, right = pairs[2 * p], pairs[2 * p + 1]
            acc[at_block(left), :] = acc[at_block(left), :] - rows[slot][0]
            acc[at_block(right), :] = acc[at_block(right), :] + rows[slot][1]
        return 0

    lax.fori_loop(0, (listed + AT_ONCE - 1) // AT_ONCE, several, 0)

    per_x = CELL_XY * CELL_Z
    groups = per_x // 8
    kz = sub % CELL_Z
    kys = [sub // CELL_Z + (8 // CELL_Z) * j for j in range(groups)]
    z_centre = (kz.astype(F32) + 0.5) / (16 * CELL_Z)
    y_centres = [(ky.astype(F32) + 0.5) / CELL_XY for ky in kys]
    m_high, m_low = split(moments[...])
    m_cols = jnp.concatenate([m_high.astype(F32), m_high.astype(F32), m_low.astype(F32)], 0).T.astype(BF16)

    def far(b, _):
        t_high, t_low = split(terms[:, at_lanes(b)])
        weight = matmul(m_cols, jnp.concatenate([t_high, t_low, t_high], 0))
        tile = main[at_block(b), :]
        mx, my, mz = (jnp.broadcast_to(tile[k : k + 1], (8, LANES)) for k in range(3))
        here = jnp.broadcast_to(cell[pl.ds(b, 1), :], (8, LANES))
        cx, cy, cz = here // per_x, here // CELL_Z % CELL_XY, here % CELL_Z
        rz = z_centre - mz
        rys = [centre - my for centre in y_centres]
        flat = [ry * ry + rz * rz + CORE_SQ for ry in rys]
        gap_z = jnp.abs(kz - cz)
        gaps = [jnp.maximum(jnp.abs(ky - cy), gap_z) for ky in kys]
        sums = [empty] * groups
        fx = empty
        for kx in range(CELL_XY):
            rx = (kx + 0.5) / CELL_XY - mx
            square = rx * rx
            gap_x = jnp.abs(cx - kx)
            plane = empty
            for j in range(groups):
                inv = lax.rsqrt(square + flat[j])
                lo = kx * per_x + 8 * j
                coef = weight[lo : lo + 8] * (inv * inv * inv)
                coef = jnp.where(jnp.maximum(gap_x, gaps[j]) >= 2, coef, 0.0)
                sums[j] = sums[j] + coef
                plane = plane + coef
            fx = fx + rx * plane
        fy, fall = empty, empty
        for j in range(groups):
            fy = fy + rys[j] * sums[j]
            fall = fall + sums[j]
        rows = empty
        for k, value in enumerate((fx, fy, rz * fall)):
            rows = jnp.where(sub == k, jnp.sum(value, 0, keepdims=True), rows)
        own_acc[at_block(b), :] = acc[at_block(b), :] + FAR_COEF * rows
        return 0

    lax.fori_loop(0, blocks, far, 0, unroll=4)
    for r in range(4):
        lo = 8 * (blocks + r * width)
        ghost_acc[r] = acc[lo : lo + 8 * width]


def finish(width, slots, counts, own_acc, returned, out, acc):
    blocks = own_acc.shape[0] // 8
    acc[...] = own_acc[...]
    for r in range(4):

        def add(g, _):
            at = at_block(slots[r * width + g])
            acc[at, :] = acc[at, :] + returned[r, at_block(g), :]
            return 0

        lax.fori_loop(0, counts[r], add, 0)

    def write(b, _):
        tile = acc[at_block(b), :]
        both = 0.5 * tile[0:3]
        out[0:3, at_lanes(b)] = both - tile[3:6]
        out[3:6, at_lanes(b)] = both + tile[3:6]
        return 0

    lax.fori_loop(0, blocks, write, 0, unroll=4)


def shape(*dims):
    return jax.ShapeDtypeStruct(dims, F32)


def on_device(sizes, ends, burgers, seg_cell, send_blocks, send_count, pair_list, pair_count):
    seg_here = ends.shape[1]
    blocks = seg_here // LANES
    width = send_blocks.shape[2]
    sent_rows = 9 * width
    (ax, nx), (ay, ny) = sizes
    slots = send_blocks.reshape(-1)
    counts = send_count.reshape(-1)
    cell = seg_cell.reshape(blocks, LANES)
    here = lax.axis_index(ax) * ny + lax.axis_index(ay)
    count = lax.dynamic_slice(pair_count, (here,), (1,))
    params = pltpu.CompilerParams(vmem_limit_bytes=VMEM_LIMIT)

    main, bz, terms, outgoing, local = pl.pallas_call(
        functools.partial(prepare, width),
        out_shape=(
            shape(blocks * 8, LANES),
            shape(blocks, LANES),
            shape(TERM_ROWS, seg_here),
            shape(4, sent_rows, LANES),
            shape(TERM_ROWS, CELLS),
        ),
        in_specs=[SMEM_SPEC] * 2 + [VMEM_SPEC] * 3,
        out_specs=(VMEM_SPEC,) * 5,
        compiler_params=params,
        name="prepare",
    )(slots, counts, ends, burgers, cell)

    dma = pltpu.SemaphoreType.DMA
    ghosts, moments = pl.pallas_call(
        functools.partial(exchange, sizes),
        out_shape=(shape(4, sent_rows, LANES), shape(TERM_ROWS, CELLS)),
        in_specs=[VMEM_SPEC] * 2,
        out_specs=(VMEM_SPEC,) * 2,
        scratch_shapes=[
            pltpu.VMEM((nx - 1, TERM_ROWS, CELLS), F32),
            pltpu.VMEM((ny - 1, TERM_ROWS, CELLS), F32),
            pltpu.VMEM((TERM_ROWS, CELLS), F32),
            dma((4,)),
            dma((4,)),
            dma((nx - 1,)),
            dma((nx - 1,)),
            dma((ny - 1,)),
            dma((ny - 1,)),
        ],
        compiler_params=pltpu.CompilerParams(
            collective_id=0, has_side_effects=True, vmem_limit_bytes=VMEM_LIMIT
        ),
        name="exchange",
    )(outgoing, local)

    own_acc, ghost_acc = pl.pallas_call(
        functools.partial(interact, width),
        out_shape=(shape(blocks * 8, LANES), shape(4, 8 * width, LANES)),
        in_specs=[SMEM_SPEC] * 2 + [VMEM_SPEC] * 6,
        out_specs=(VMEM_SPEC,) * 2,
        scratch_shapes=[pltpu.VMEM(((blocks + 4 * width) * 8, LANES), F32)] * 3
        + [
            pltpu.VMEM((AT_ONCE, 80, 8 * LANES), BF16),
            pltpu.VMEM((AT_ONCE, LANES, 8 * LANES), F32),
            pltpu.VMEM((AT_ONCE, LANES, 12 * LANES), BF16),
        ],
        compiler_params=params,
        name="interact",
    )(pair_list.reshape(-1), count, main, bz, ghosts, cell, terms, moments)

    returned = pl.pallas_call(
        functools.partial(give_back, sizes),
        out_shape=shape(4, 8 * width, LANES),
        in_specs=[VMEM_SPEC],
        out_specs=VMEM_SPEC,
        scratch_shapes=[dma((4,)), dma((4,))],
        compiler_params=pltpu.CompilerParams(
            collective_id=1, has_side_effects=True, vmem_limit_bytes=VMEM_LIMIT
        ),
        name="give_back",
    )(ghost_acc)

    return pl.pallas_call(
        functools.partial(finish, width),
        out_shape=shape(6, seg_here),
        in_specs=[SMEM_SPEC] * 2 + [VMEM_SPEC] * 2,
        out_specs=VMEM_SPEC,
        scratch_shapes=[pltpu.VMEM((blocks * 8, LANES), F32)],
        compiler_params=params,
        name="finish",
    )(slots, counts, own_acc, returned)


def solution(mesh):
    sizes = (("gx", mesh.shape["gx"]), ("gy", mesh.shape["gy"]))
    return jax.shard_map(
        functools.partial(on_device, sizes),
        mesh=mesh,
        in_specs=(
            P(None, ("gx", "gy")),
            P(None, ("gx", "gy")),
            P(("gx", "gy")),
            P(("gx", "gy"), None, None),
            P(("gx", "gy"), None),
            P(("gx", "gy"), None, None),
            P(),
        ),
        out_specs=P(None, ("gx", "gy")),
        check_vma=False,
    )
```

```python
import functools

import jax
import jax.numpy as jnp
from jax import lax
from jax.experimental import pallas as pl
from jax.experimental.pallas import tpu as pltpu
from jax.sharding import PartitionSpec as P

CELL_XY = 8
CELL_Z = 4
CELLS = 256
LANES = 128
TERM_ROWS = 16
CHUNK = 1024
AT_ONCE = 4

CORE_SQ = 2.5e-05
NEAR_COEF = 0.2
FAR_COEF = 0.2
F32 = jnp.float32
BF16 = jnp.bfloat16
MESH = pl.DeviceIdType.MESH
VMEM_SPEC = pl.BlockSpec(memory_space=pltpu.VMEM)
SMEM_SPEC = pl.BlockSpec(memory_space=pltpu.SMEM)
VMEM_LIMIT = 48 * 1024 * 1024


def split(value):
    high = value.astype(BF16)
    return high, (value - high.astype(F32)).astype(BF16)


def matmul(a, b):
    return jnp.dot(a, b, preferred_element_type=F32)


def at_block(index, rows=8):
    return pl.ds(pl.multiple_of(index * rows, rows), rows)


def at_lanes(index, lanes=LANES):
    return pl.ds(pl.multiple_of(index * lanes, lanes), lanes)


def prepare(width, slots, counts, ends, burgers, cell, main, bz, terms, outgoing, moments):
    blocks = main.shape[0] // 8

    def rows(b, _):
        at = at_lanes(b)
        first, second, burg = ends[0:3, at], ends[3:6, at], burgers[:, at]
        line = second - first
        base = pl.multiple_of(b * 8, 8)
        main[pl.ds(base, 3), :] = 0.5 * (first + second)
        main[pl.ds(base + 3, 3), :] = line
        main[pl.ds(base + 6, 2), :] = burg[0:2]
        bz[pl.ds(b, 1), :] = burg[2:3]
        for p in range(3):
            terms[3 * p : 3 * p + 3, at] = burg[p : p + 1] * line
        terms[9:12, at] = line
        terms[12:16, at] = jnp.zeros((4, LANES), F32)
        return 0

    lax.fori_loop(0, blocks, rows, 0, unroll=4)

    for r in range(4):

        def gather(g, _):
            block = slots[r * width + g]
            keep = jnp.where(g < counts[r], 1.0, 0.0).astype(F32)
            outgoing[r, at_block(g), :] = main[at_block(block), :] * keep
            outgoing[r, pl.ds(8 * width + g, 1), :] = bz[pl.ds(block, 1), :] * keep
            return 0

        lax.fori_loop(0, width, gather, 0, unroll=4)

    per = CHUNK // LANES
    ids = lax.broadcasted_iota(jnp.int32, (CELLS, LANES), 0)

    def add(c, total):
        at = at_lanes(c, CHUNK)
        high, low = split(terms[:, at])
        both = jnp.concatenate([high, low], 0)
        hot = jnp.concatenate(
            [jnp.where(cell[pl.ds(c * per + k, 1), :] == ids, 1.0, 0.0).astype(BF16) for k in range(per)], 1
        )
        return total + lax.dot_general(both, hot, (((1,), (1,)), ((), ())), preferred_element_type=F32)

    total = lax.fori_loop(0, blocks // per, add, jnp.zeros((2 * TERM_ROWS, CELLS), F32))
    moments[...] = total[:TERM_ROWS] + total[TERM_ROWS:]


def hello(sizes):
    barrier = pltpu.get_barrier_semaphore()
    for axis, size in sizes:
        me = lax.axis_index(axis)
        for step in range(1, size):
            pl.semaphore_signal(
                barrier, inc=1, device_id={axis: lax.rem(me + step, size)}, device_id_type=MESH
            )
    pl.semaphore_wait(barrier, sum(size - 1 for _, size in sizes))


def hello_near(sizes):
    barrier = pltpu.get_barrier_semaphore()
    peers = 0
    for axis, size in sizes:
        me = lax.axis_index(axis)
        peers = peers + jnp.where(me > 0, 1, 0) + jnp.where(me < size - 1, 1, 0)
        for step in (-1, 1):
            there = me > 0 if step < 0 else me < size - 1

            @pl.when(there)
            def _():
                pl.semaphore_signal(barrier, inc=1, device_id={axis: me + step}, device_id_type=MESH)

    pl.semaphore_wait(barrier, peers)


def neighbours(sizes, source, target, send_sem, recv_sem):
    out = []
    for r in range(4):
        axis, size = sizes[r // 2]
        me = lax.axis_index(axis)
        step = 1 if r % 2 else -1
        there = me < size - 1 if r % 2 else me > 0
        peer = jnp.clip(me + step, 0, size - 1)
        copy = pltpu.make_async_remote_copy(
            src_ref=source.at[r],
            dst_ref=target.at[r ^ 1],
            send_sem=send_sem.at[r],
            recv_sem=recv_sem.at[r ^ 1],
            device_id={axis: peer},
            device_id_type=MESH,
        )
        back = pltpu.make_async_remote_copy(
            src_ref=source.at[r],
            dst_ref=target.at[r],
            send_sem=send_sem.at[r],
            recv_sem=recv_sem.at[r],
            device_id={axis: peer},
            device_id_type=MESH,
        )
        out.append((there, copy, back))
    return out


def start_all(copies, target):
    for r, (there, copy, _) in enumerate(copies):

        @pl.when(there)
        def _():
            copy.start()

        @pl.when(jnp.logical_not(there))
        def _():
            target[r] = jnp.zeros(target.shape[1:], F32)


def wait_all(copies):
    for there, copy, back in copies:

        @pl.when(there)
        def _():
            copy.wait_send()
            back.wait_recv()


def exchange(sizes, outgoing, local, ghosts, moments, held_x, held_y, partial, send_sem, recv_sem, sx, rx, sy, ry):
    hello(sizes)
    (ax, nx), (ay, ny) = sizes

    def spread(source, axis, size, held, send, recv):
        me = lax.axis_index(axis)
        copies = []
        for step in range(1, size):
            copy = pltpu.make_async_remote_copy(
                src_ref=source,
                dst_ref=held.at[step - 1],
                send_sem=send.at[step - 1],
                recv_sem=recv.at[step - 1],
                device_id={axis: lax.rem(me + step, size)},
                device_id_type=MESH,
            )
            copy.start()
            copies.append(copy)
        return copies

    first = spread(local, ay, ny, held_y, sy, ry)
    copies = neighbours(sizes, outgoing, ghosts, send_sem, recv_sem)
    start_all(copies, ghosts)
    total = local[...]
    for k, copy in enumerate(first):
        copy.wait()
        total = total + held_y[k]
    partial[...] = total
    second = spread(partial, ax, nx, held_x, sx, rx)
    for k, copy in enumerate(second):
        copy.wait()
        total = total + held_x[k]
    moments[...] = total
    wait_all(copies)


def far_forces(main, cell, terms, moments, forces):
    blocks = main.shape[0] // 8
    sub = lax.broadcasted_iota(jnp.int32, (8, LANES), 0)
    empty = jnp.zeros((8, LANES), F32)
    per_x = CELL_XY * CELL_Z
    groups = per_x // 8
    kz = sub % CELL_Z
    kys = [sub // CELL_Z + (8 // CELL_Z) * j for j in range(groups)]
    z_centre = (kz.astype(F32) + 0.5) / (16 * CELL_Z)
    y_centres = [(ky.astype(F32) + 0.5) / CELL_XY for ky in kys]
    m_high, m_low = split(moments[...])
    m_cols = jnp.concatenate([m_high.astype(F32), m_high.astype(F32), m_low.astype(F32)], 0).T.astype(BF16)

    def far(b, _):
        t_high, t_low = split(terms[:, at_lanes(b)])
        weight = matmul(m_cols, jnp.concatenate([t_high, t_low, t_high], 0))
        tile = main[at_block(b), :]
        mx, my, mz = (jnp.broadcast_to(tile[k : k + 1], (8, LANES)) for k in range(3))
        here = jnp.broadcast_to(cell[pl.ds(b, 1), :], (8, LANES))
        cx, cy, cz = here // per_x, here // CELL_Z % CELL_XY, here % CELL_Z
        rz = z_centre - mz
        rys = [centre - my for centre in y_centres]
        flat = [ry * ry + rz * rz + CORE_SQ for ry in rys]
        gap_z = jnp.abs(kz - cz)
        gaps = [jnp.maximum(jnp.abs(ky - cy), gap_z) for ky in kys]
        sums = [empty] * groups
        fx = empty
        for kx in range(CELL_XY):
            rx = (kx + 0.5) / CELL_XY - mx
            square = rx * rx
            gap_x = jnp.abs(cx - kx)
            plane = empty
            for j in range(groups):
                inv = lax.rsqrt(square + flat[j])
                lo = kx * per_x + 8 * j
                coef = weight[lo : lo + 8] * (inv * inv * inv)
                coef = jnp.where(jnp.maximum(gap_x, gaps[j]) >= 2, coef, 0.0)
                sums[j] = sums[j] + coef
                plane = plane + coef
            fx = fx + rx * plane
        fy, fall = empty, empty
        for j in range(groups):
            fy = fy + rys[j] * sums[j]
            fall = fall + sums[j]
        rows = empty
        for k, value in enumerate((fx, fy, rz * fall)):
            rows = jnp.where(sub == k, jnp.sum(value, 0, keepdims=True), rows)
        forces[at_block(b), :] = FAR_COEF * rows
        return 0

    lax.fori_loop(0, blocks, far, 0, unroll=4)


def give_back(sizes, forces, main, cell, terms, moments, returned, far, send_sem, recv_sem):
    hello_near(sizes)
    copies = neighbours(sizes, forces, returned, send_sem, recv_sem)
    start_all(copies, returned)
    far_forces(main, cell, terms, moments, far)
    wait_all(copies)


def interact(
    sizes, width, pairs, counts, main, bz, ghosts, own_acc, ghost_acc, ext, sym, acc, rhs, wide, xs
):
    blocks = main.shape[0] // 8
    total = blocks + 4 * width
    acc[...] = jnp.zeros_like(acc)
    ext[0 : 8 * blocks] = main[...]
    for r in range(4):
        lo = 8 * (blocks + r * width)
        ext[lo : lo + 8 * width] = ghosts[r, 0 : 8 * width]

    def products(first, many, burg_z):
        def row(k):
            return pl.ds(8 * first + k, many, stride=8)

        lx, ly, lz, bx, by = (ext[row(k), :] for k in (3, 4, 5, 6, 7))
        sym[row(0), :] = 2.0 * bx * lx
        sym[row(1), :] = 2.0 * by * ly
        sym[row(2), :] = 2.0 * burg_z * lz
        sym[row(3), :] = bx * ly + by * lx
        sym[row(4), :] = bx * lz + burg_z * lx
        sym[row(5), :] = by * lz + burg_z * ly
        zero = jnp.zeros((many, LANES), F32)
        sym[row(6), :] = zero
        sym[row(7), :] = zero
        ext[row(6), :] = lx * lx + ly * ly + lz * lz

    for b in range(0, blocks, 8):
        products(b, 8, bz[b : b + 8])
    for r in range(4):
        for g in range(0, width, 8):
            products(blocks + r * width + g, 8, ghosts[r, 8 * width + g : 8 * width + g + 8])

    sub = lax.broadcasted_iota(jnp.int32, (8, LANES), 0)
    ahead = lax.broadcasted_iota(jnp.int32, (16, LANES), 1) - lax.broadcasted_iota(jnp.int32, (16, LANES), 0)
    scale = jnp.where(sub < 3, 0.5 * NEAR_COEF, jnp.where(sub < 6, NEAR_COEF, 0.0)).astype(F32)
    empty = jnp.zeros((8, LANES), F32)
    (ax, _), (ay, ny) = sizes
    listed = counts[lax.axis_index(ax) * ny + lax.axis_index(ay)]

    def parts(value, many):
        out = []
        for _ in range(many):
            part = value.astype(BF16).astype(F32)
            out.append(part)
            value = value - part
        return out

    depth, across = rhs.shape[1:]
    row = lax.broadcasted_iota(jnp.int32, (depth, across), 0)
    out_id = lax.broadcasted_iota(jnp.int32, (depth, across), 1) // LANES - 1
    pick = jnp.where(out_id < 3, -1.0, 1.0)
    pattern = jnp.where(jnp.logical_and(row < 24, row % 8 == out_id), pick, 0.0).astype(BF16)
    for slot in range(AT_ONCE):
        rhs[slot] = pattern
    ones = jnp.ones((8, LANES), F32)
    edge = [jnp.where(sub == k, -1.0, 0.0).astype(F32) for k in range(3)]
    summed = xs.shape[2]
    adder = jnp.where(
        lax.broadcasted_iota(jnp.int32, (8, summed), 1) // (2 * LANES)
        == lax.broadcasted_iota(jnp.int32, (8, summed), 0),
        1.0,
        0.0,
    ).astype(BF16)

    def turn(slot, p):
        left, right = pairs[2 * p], pairs[2 * p + 1]
        s_high, s_low = parts(sym[at_block(left), :], 2)
        t_high, t_low = parts(sym[at_block(right), :] * scale, 2)
        own = parts(ext[at_block(left), :], 3)
        other = parts(ext[at_block(right), :], 3)
        col = jnp.concatenate(own + [ones] * 3 + [s_high, s_high, s_low, empty], 0).T
        rhs[slot, 48:80, 0:LANES] = jnp.concatenate([t_high, t_low, t_high, empty], 0).astype(BF16)
        for k in range(3):
            keep = jnp.where(sub == k, 1.0, 0.0)
            rows = jnp.concatenate([edge[k]] + [part * keep for part in other], 0)
            rhs[slot, 16:48, (k + 1) * LANES : (k + 2) * LANES] = rows.astype(BF16)
        wide[slot] = matmul(col.astype(BF16), rhs[slot])

    def forces(slot, p):
        left, right = pairs[2 * p], pairs[2 * p + 1]
        floor = jnp.where(left == right, 0, -1024)
        floor = jnp.where(p < listed, floor, 1024)
        tile_t = ext[at_block(right), :]
        lt = [tile_t[k + 3 : k + 4] for k in range(3)]
        len_t = tile_t[6:7]
        sums_t = [jnp.zeros((8, LANES), F32)] * 6
        for c in range(LANES // 16):
            lo = 16 * c
            known = [wide[slot, lo : lo + 16, k * LANES : (k + 1) * LANES] for k in range(8)]
            rel, ls, len_s = known[1:4], known[4:7], known[7]
            quad = rel[0] * rel[0] + rel[1] * rel[1] + rel[2] * rel[2] + CORE_SQ
            inv = lax.rsqrt(quad)
            coef = known[0] * (inv * inv * inv)
            coef = jnp.where(ahead > floor + lo, coef, 0.0)
            push = [coef * rel[k] for k in range(3)]
            along_s = ls[0] * rel[0] + ls[1] * rel[1] + ls[2] * rel[2]
            along_t = lt[0] * rel[0] + lt[1] * rel[1] + lt[2] * rel[2]
            den_s = quad + len_s
            den_t = quad + len_t
            both = den_s * den_t
            near = pl.reciprocal(both, approx=True)
            near = near * (2.0 - both * near)
            half = 0.5 * near
            share_s = along_s * den_t * half
            share_t = along_t * den_s * half
            for k in range(3):
                skew = share_t * push[k]
                sums_t[k] = sums_t[k] + (push[k][0:8] + push[k][8:16])
                sums_t[k + 3] = sums_t[k + 3] - (skew[0:8] + skew[8:16])
            for k, value in enumerate(push + [share_s * push[k] for k in range(3)]):
                high, low = split(value)
                xs[slot, lo : lo + 16, 2 * k * LANES : (2 * k + 1) * LANES] = high
                xs[slot, lo : lo + 16, (2 * k + 1) * LANES : (2 * k + 2) * LANES] = low
        rows_t = empty
        for k in range(6):
            rows_t = jnp.where(sub == k, jnp.sum(sums_t[k], 0, keepdims=True), rows_t)
        rows_s = lax.dot_general(adder, xs[slot], (((1,), (1,)), ((), ())), preferred_element_type=F32)
        return rows_s, rows_t

    def several(q, _):
        group = [(slot, q * AT_ONCE + slot) for slot in range(AT_ONCE)]
        for slot, p in group:
            turn(slot, p)
        rows = [forces(slot, p) for slot, p in group]
        for slot, p in group:
            left, right = pairs[2 * p], pairs[2 * p + 1]
            acc[at_block(left), :] = acc[at_block(left), :] - rows[slot][0]
            acc[at_block(right), :] = acc[at_block(right), :] + rows[slot][1]
        return 0

    lax.fori_loop(0, (listed + AT_ONCE - 1) // AT_ONCE, several, 0)

    own_acc[...] = acc[0 : 8 * blocks]
    for r in range(4):
        lo = 8 * (blocks + r * width)
        ghost_acc[r] = acc[lo : lo + 8 * width]


def finish(width, slots, counts, own_acc, returned, far, out, acc):
    blocks = own_acc.shape[0] // 8
    acc[...] = own_acc[...] + far[...]
    for r in range(4):

        def add(g, _):
            at = at_block(slots[r * width + g])
            acc[at, :] = acc[at, :] + returned[r, at_block(g), :]
            return 0

        lax.fori_loop(0, counts[r], add, 0)

    def write(b, _):
        tile = acc[at_block(b), :]
        both = 0.5 * tile[0:3]
        out[0:3, at_lanes(b)] = both - tile[3:6]
        out[3:6, at_lanes(b)] = both + tile[3:6]
        return 0

    lax.fori_loop(0, blocks, write, 0, unroll=4)


def shape(*dims):
    return jax.ShapeDtypeStruct(dims, F32)


def on_device(sizes, ends, burgers, seg_cell, send_blocks, send_count, pair_list, pair_count):
    seg_here = ends.shape[1]
    blocks = seg_here // LANES
    width = send_blocks.shape[2]
    sent_rows = 9 * width
    (ax, nx), (ay, ny) = sizes
    slots = send_blocks.reshape(-1)
    counts = send_count.reshape(-1)
    cell = seg_cell.reshape(blocks, LANES)
    params = pltpu.CompilerParams(vmem_limit_bytes=VMEM_LIMIT)

    main, bz, terms, outgoing, local = pl.pallas_call(
        functools.partial(prepare, width),
        out_shape=(
            shape(blocks * 8, LANES),
            shape(blocks, LANES),
            shape(TERM_ROWS, seg_here),
            shape(4, sent_rows, LANES),
            shape(TERM_ROWS, CELLS),
        ),
        in_specs=[SMEM_SPEC] * 2 + [VMEM_SPEC] * 3,
        out_specs=(VMEM_SPEC,) * 5,
        compiler_params=params,
        name="prepare",
    )(slots, counts, ends, burgers, cell)

    dma = pltpu.SemaphoreType.DMA
    ghosts, moments = pl.pallas_call(
        functools.partial(exchange, sizes),
        out_shape=(shape(4, sent_rows, LANES), shape(TERM_ROWS, CELLS)),
        in_specs=[VMEM_SPEC] * 2,
        out_specs=(VMEM_SPEC,) * 2,
        scratch_shapes=[
            pltpu.VMEM((nx - 1, TERM_ROWS, CELLS), F32),
            pltpu.VMEM((ny - 1, TERM_ROWS, CELLS), F32),
            pltpu.VMEM((TERM_ROWS, CELLS), F32),
            dma((4,)),
            dma((4,)),
            dma((nx - 1,)),
            dma((nx - 1,)),
            dma((ny - 1,)),
            dma((ny - 1,)),
        ],
        compiler_params=pltpu.CompilerParams(
            collective_id=0, has_side_effects=True, vmem_limit_bytes=VMEM_LIMIT
        ),
        name="exchange",
    )(outgoing, local)

    own_acc, ghost_acc = pl.pallas_call(
        functools.partial(interact, sizes, width),
        out_shape=(shape(blocks * 8, LANES), shape(4, 8 * width, LANES)),
        in_specs=[SMEM_SPEC] * 2 + [VMEM_SPEC] * 3,
        out_specs=(VMEM_SPEC,) * 2,
        scratch_shapes=[pltpu.VMEM(((blocks + 4 * width) * 8, LANES), F32)] * 3
        + [
            pltpu.VMEM((AT_ONCE, 80, 8 * LANES), BF16),
            pltpu.VMEM((AT_ONCE, LANES, 8 * LANES), F32),
            pltpu.VMEM((AT_ONCE, LANES, 12 * LANES), BF16),
        ],
        compiler_params=params,
        name="interact",
    )(pair_list.reshape(-1), pair_count, main, bz, ghosts)

    returned, far = pl.pallas_call(
        functools.partial(give_back, sizes),
        out_shape=(shape(4, 8 * width, LANES), shape(blocks * 8, LANES)),
        in_specs=[VMEM_SPEC] * 5,
        out_specs=(VMEM_SPEC,) * 2,
        scratch_shapes=[dma((4,)), dma((4,))],
        compiler_params=pltpu.CompilerParams(
            collective_id=1, has_side_effects=True, vmem_limit_bytes=VMEM_LIMIT
        ),
        name="give_back",
    )(ghost_acc, main, cell, terms, moments)

    return pl.pallas_call(
        functools.partial(finish, width),
        out_shape=shape(6, seg_here),
        in_specs=[SMEM_SPEC] * 2 + [VMEM_SPEC] * 3,
        out_specs=VMEM_SPEC,
        scratch_shapes=[pltpu.VMEM((blocks * 8, LANES), F32)],
        compiler_params=params,
        name="finish",
    )(slots, counts, own_acc, returned, far)


def solution(mesh):
    sizes = (("gx", mesh.shape["gx"]), ("gy", mesh.shape["gy"]))
    return jax.shard_map(
        functools.partial(on_device, sizes),
        mesh=mesh,
        in_specs=(
            P(None, ("gx", "gy")),
            P(None, ("gx", "gy")),
            P(("gx", "gy")),
            P(("gx", "gy"), None, None),
            P(("gx", "gy"), None),
            P(("gx", "gy"), None, None),
            P(),
        ),
        out_specs=P(None, ("gx", "gy")),
        check_vma=False,
    )
```

```python
import functools

import jax
import jax.numpy as jnp
from jax import lax
from jax.experimental import pallas as pl
from jax.experimental.pallas import tpu as pltpu
from jax.sharding import PartitionSpec as P

CELL_XY = 8
CELL_Z = 4
CELLS = 256
LANES = 128
TERM_ROWS = 16
CHUNK = 1024
AT_ONCE = 8

CORE_SQ = 2.5e-05
NEAR_COEF = 0.2
FAR_COEF = 0.2
F32 = jnp.float32
BF16 = jnp.bfloat16
MESH = pl.DeviceIdType.MESH
VMEM_SPEC = pl.BlockSpec(memory_space=pltpu.VMEM)
SMEM_SPEC = pl.BlockSpec(memory_space=pltpu.SMEM)
VMEM_LIMIT = 48 * 1024 * 1024


def split(value):
    high = value.astype(BF16)
    return high, (value - high.astype(F32)).astype(BF16)


def matmul(a, b):
    return jnp.dot(a, b, preferred_element_type=F32)


def at_block(index, rows=8):
    return pl.ds(pl.multiple_of(index * rows, rows), rows)


def at_lanes(index, lanes=LANES):
    return pl.ds(pl.multiple_of(index * lanes, lanes), lanes)


def prepare(width, slots, counts, ends, burgers, main, bz, terms, outgoing):
    blocks = main.shape[0] // 8

    def rows(b, _):
        at = at_lanes(b)
        first, second, burg = ends[0:3, at], ends[3:6, at], burgers[:, at]
        line = second - first
        base = pl.multiple_of(b * 8, 8)
        main[pl.ds(base, 3), :] = 0.5 * (first + second)
        main[pl.ds(base + 3, 3), :] = line
        main[pl.ds(base + 6, 2), :] = burg[0:2]
        bz[pl.ds(b, 1), :] = burg[2:3]
        for p in range(3):
            terms[3 * p : 3 * p + 3, at] = burg[p : p + 1] * line
        terms[9:12, at] = line
        terms[12:16, at] = jnp.zeros((4, LANES), F32)
        return 0

    lax.fori_loop(0, blocks, rows, 0, unroll=4)

    for r in range(4):

        def gather(g, _):
            block = slots[r * width + g]
            keep = jnp.where(g < counts[r], 1.0, 0.0).astype(F32)
            outgoing[r, at_block(g), :] = main[at_block(block), :] * keep
            outgoing[r, pl.ds(8 * width + g, 1), :] = bz[pl.ds(block, 1), :] * keep
            return 0

        lax.fori_loop(0, width, gather, 0, unroll=4)


def local_moments(cell, terms, moments):
    blocks = cell.shape[0]
    per = CHUNK // LANES
    ids = lax.broadcasted_iota(jnp.int32, (CELLS, LANES), 0)

    def add(c, total):
        at = at_lanes(c, CHUNK)
        high, low = split(terms[:, at])
        both = jnp.concatenate([high, low], 0)
        hot = jnp.concatenate(
            [jnp.where(cell[pl.ds(c * per + k, 1), :] == ids, 1.0, 0.0).astype(BF16) for k in range(per)], 1
        )
        return total + lax.dot_general(both, hot, (((1,), (1,)), ((), ())), preferred_element_type=F32)

    total = lax.fori_loop(0, blocks // per, add, jnp.zeros((2 * TERM_ROWS, CELLS), F32))
    moments[...] = total[:TERM_ROWS] + total[TERM_ROWS:]


def hello(sizes):
    barrier = pltpu.get_barrier_semaphore()
    for axis, size in sizes:
        me = lax.axis_index(axis)
        for step in range(1, size):
            pl.semaphore_signal(
                barrier, inc=1, device_id={axis: lax.rem(me + step, size)}, device_id_type=MESH
            )
    pl.semaphore_wait(barrier, sum(size - 1 for _, size in sizes))


def hello_near(sizes):
    barrier = pltpu.get_barrier_semaphore()
    peers = 0
    for axis, size in sizes:
        me = lax.axis_index(axis)
        peers = peers + jnp.where(me > 0, 1, 0) + jnp.where(me < size - 1, 1, 0)
        for step in (-1, 1):
            there = me > 0 if step < 0 else me < size - 1

            @pl.when(there)
            def _():
                pl.semaphore_signal(barrier, inc=1, device_id={axis: me + step}, device_id_type=MESH)

    pl.semaphore_wait(barrier, peers)


def neighbours(sizes, source, target, send_sem, recv_sem):
    out = []
    for r in range(4):
        axis, size = sizes[r // 2]
        me = lax.axis_index(axis)
        step = 1 if r % 2 else -1
        there = me < size - 1 if r % 2 else me > 0
        peer = jnp.clip(me + step, 0, size - 1)
        copy = pltpu.make_async_remote_copy(
            src_ref=source.at[r],
            dst_ref=target.at[r ^ 1],
            send_sem=send_sem.at[r],
            recv_sem=recv_sem.at[r ^ 1],
            device_id={axis: peer},
            device_id_type=MESH,
        )
        back = pltpu.make_async_remote_copy(
            src_ref=source.at[r],
            dst_ref=target.at[r],
            send_sem=send_sem.at[r],
            recv_sem=recv_sem.at[r],
            device_id={axis: peer},
            device_id_type=MESH,
        )
        out.append((there, copy, back))
    return out


def start_all(copies, target):
    for r, (there, copy, _) in enumerate(copies):

        @pl.when(there)
        def _():
            copy.start()

        @pl.when(jnp.logical_not(there))
        def _():
            target[r] = jnp.zeros(target.shape[1:], F32)


def wait_all(copies):
    for there, copy, back in copies:

        @pl.when(there)
        def _():
            copy.wait_send()
            back.wait_recv()


def exchange(sizes, outgoing, cell, terms, ghosts, moments, local, held_x, held_y, partial, send_sem, recv_sem, sx, rx, sy, ry):
    hello(sizes)
    (ax, nx), (ay, ny) = sizes

    def spread(source, axis, size, held, send, recv):
        me = lax.axis_index(axis)
        copies = []
        for step in range(1, size):
            copy = pltpu.make_async_remote_copy(
                src_ref=source,
                dst_ref=held.at[step - 1],
                send_sem=send.at[step - 1],
                recv_sem=recv.at[step - 1],
                device_id={axis: lax.rem(me + step, size)},
                device_id_type=MESH,
            )
            copy.start()
            copies.append(copy)
        return copies

    copies = neighbours(sizes, outgoing, ghosts, send_sem, recv_sem)
    start_all(copies, ghosts)
    local_moments(cell, terms, local)
    first = spread(local, ay, ny, held_y, sy, ry)
    total = local[...]
    for k, copy in enumerate(first):
        copy.wait()
        total = total + held_y[k]
    partial[...] = total
    second = spread(partial, ax, nx, held_x, sx, rx)
    for k, copy in enumerate(second):
        copy.wait()
        total = total + held_x[k]
    moments[...] = total
    wait_all(copies)


def far_forces(main, cell, terms, moments, forces):
    blocks = main.shape[0] // 8
    sub = lax.broadcasted_iota(jnp.int32, (8, LANES), 0)
    empty = jnp.zeros((8, LANES), F32)
    per_x = CELL_XY * CELL_Z
    groups = per_x // 8
    kz = sub % CELL_Z
    kys = [sub // CELL_Z + (8 // CELL_Z) * j for j in range(groups)]
    z_centre = (kz.astype(F32) + 0.5) / (16 * CELL_Z)
    y_centres = [(ky.astype(F32) + 0.5) / CELL_XY for ky in kys]
    m_high, m_low = split(moments[...])
    m_cols = jnp.concatenate([m_high.astype(F32), m_high.astype(F32), m_low.astype(F32)], 0).T.astype(BF16)

    def far(b, _):
        t_high, t_low = split(terms[:, at_lanes(b)])
        weight = matmul(m_cols, jnp.concatenate([t_high, t_low, t_high], 0))
        tile = main[at_block(b), :]
        mx, my, mz = (jnp.broadcast_to(tile[k : k + 1], (8, LANES)) for k in range(3))
        here = jnp.broadcast_to(cell[pl.ds(b, 1), :], (8, LANES))
        cx, cy, cz = here // per_x, here // CELL_Z % CELL_XY, here % CELL_Z
        rz = z_centre - mz
        rys = [centre - my for centre in y_centres]
        flat = [ry * ry + rz * rz + CORE_SQ for ry in rys]
        gap_z = jnp.abs(kz - cz)
        gaps = [jnp.maximum(jnp.abs(ky - cy), gap_z) for ky in kys]
        sums = [empty] * groups
        fx = empty
        for kx in range(CELL_XY):
            rx = (kx + 0.5) / CELL_XY - mx
            square = rx * rx
            gap_x = jnp.abs(cx - kx)
            plane = empty
            for j in range(groups):
                inv = lax.rsqrt(square + flat[j])
                lo = kx * per_x + 8 * j
                coef = weight[lo : lo + 8] * (inv * inv * inv)
                coef = jnp.where(jnp.maximum(gap_x, gaps[j]) >= 2, coef, 0.0)
                sums[j] = sums[j] + coef
                plane = plane + coef
            fx = fx + rx * plane
        fy, fall = empty, empty
        for j in range(groups):
            fy = fy + rys[j] * sums[j]
            fall = fall + sums[j]
        rows = empty
        for k, value in enumerate((fx, fy, rz * fall)):
            rows = jnp.where(sub == k, jnp.sum(value, 0, keepdims=True), rows)
        forces[at_block(b), :] = FAR_COEF * rows
        return 0

    lax.fori_loop(0, blocks, far, 0, unroll=4)


def give_back(sizes, forces, main, cell, terms, moments, returned, far, send_sem, recv_sem):
    hello_near(sizes)
    copies = neighbours(sizes, forces, returned, send_sem, recv_sem)
    start_all(copies, returned)
    far_forces(main, cell, terms, moments, far)
    wait_all(copies)


def interact(
    sizes, width, pairs, counts, main, bz, ghosts, own_acc, ghost_acc, ext, sym, acc, rhs, wide, xs
):
    blocks = main.shape[0] // 8
    total = blocks + 4 * width
    acc[...] = jnp.zeros_like(acc)
    ext[0 : 8 * blocks] = main[...]
    for r in range(4):
        lo = 8 * (blocks + r * width)
        ext[lo : lo + 8 * width] = ghosts[r, 0 : 8 * width]

    def products(first, many, burg_z):
        def row(k):
            return pl.ds(8 * first + k, many, stride=8)

        lx, ly, lz, bx, by = (ext[row(k), :] for k in (3, 4, 5, 6, 7))
        sym[row(0), :] = 2.0 * bx * lx
        sym[row(1), :] = 2.0 * by * ly
        sym[row(2), :] = 2.0 * burg_z * lz
        sym[row(3), :] = bx * ly + by * lx
        sym[row(4), :] = bx * lz + burg_z * lx
        sym[row(5), :] = by * lz + burg_z * ly
        zero = jnp.zeros((many, LANES), F32)
        sym[row(6), :] = zero
        sym[row(7), :] = zero
        ext[row(6), :] = lx * lx + ly * ly + lz * lz

    for b in range(0, blocks, 8):
        products(b, 8, bz[b : b + 8])
    for r in range(4):
        for g in range(0, width, 8):
            products(blocks + r * width + g, 8, ghosts[r, 8 * width + g : 8 * width + g + 8])

    sub = lax.broadcasted_iota(jnp.int32, (8, LANES), 0)
    ahead = lax.broadcasted_iota(jnp.int32, (16, LANES), 1) - lax.broadcasted_iota(jnp.int32, (16, LANES), 0)
    scale = jnp.where(sub < 3, 0.5 * NEAR_COEF, jnp.where(sub < 6, NEAR_COEF, 0.0)).astype(F32)
    empty = jnp.zeros((8, LANES), F32)
    (ax, _), (ay, ny) = sizes
    listed = counts[lax.axis_index(ax) * ny + lax.axis_index(ay)]

    def parts(value, many):
        out = []
        for _ in range(many):
            part = value.astype(BF16).astype(F32)
            out.append(part)
            value = value - part
        return out

    depth, across = rhs.shape[1:]
    row = lax.broadcasted_iota(jnp.int32, (depth, across), 0)
    out_id = lax.broadcasted_iota(jnp.int32, (depth, across), 1) // LANES - 1
    pick = jnp.where(out_id < 3, -1.0, 1.0)
    pattern = jnp.where(jnp.logical_and(row < 24, row % 8 == out_id), pick, 0.0).astype(BF16)
    for slot in range(AT_ONCE):
        rhs[slot] = pattern
    ones = jnp.ones((8, LANES), F32)
    edge = [jnp.where(sub == k, -1.0, 0.0).astype(F32) for k in range(3)]
    summed = xs.shape[2]
    adder = jnp.where(
        lax.broadcasted_iota(jnp.int32, (8, summed), 1) // (2 * LANES)
        == lax.broadcasted_iota(jnp.int32, (8, summed), 0),
        1.0,
        0.0,
    ).astype(BF16)

    def turn(slot, p):
        left, right = pairs[2 * p], pairs[2 * p + 1]
        s_high, s_low = parts(sym[at_block(left), :], 2)
        t_high, t_low = parts(sym[at_block(right), :] * scale, 2)
        own = parts(ext[at_block(left), :], 3)
        other = parts(ext[at_block(right), :], 3)
        col = jnp.concatenate(own + [ones] * 3 + [s_high, s_high, s_low, empty], 0).T
        rhs[slot, 48:80, 0:LANES] = jnp.concatenate([t_high, t_low, t_high, empty], 0).astype(BF16)
        for k in range(3):
            keep = jnp.where(sub == k, 1.0, 0.0)
            rows = jnp.concatenate([edge[k]] + [part * keep for part in other], 0)
            rhs[slot, 16:48, (k + 1) * LANES : (k + 2) * LANES] = rows.astype(BF16)
        wide[slot] = matmul(col.astype(BF16), rhs[slot])

    def forces(slot, p):
        left, right = pairs[2 * p], pairs[2 * p + 1]
        floor = jnp.where(left == right, 0, -1024)
        floor = jnp.where(p < listed, floor, 1024)
        tile_t = ext[at_block(right), :]
        lt = [tile_t[k + 3 : k + 4] for k in range(3)]
        len_t = tile_t[6:7]
        sums_t = [jnp.zeros((8, LANES), F32)] * 6
        for c in range(LANES // 16):
            lo = 16 * c
            known = [wide[slot, lo : lo + 16, k * LANES : (k + 1) * LANES] for k in range(8)]
            rel, ls, len_s = known[1:4], known[4:7], known[7]
            quad = rel[0] * rel[0] + rel[1] * rel[1] + rel[2] * rel[2] + CORE_SQ
            inv = lax.rsqrt(quad)
            coef = known[0] * (inv * inv * inv)
            coef = jnp.where(ahead > floor + lo, coef, 0.0)
            push = [coef * rel[k] for k in range(3)]
            along_s = ls[0] * rel[0] + ls[1] * rel[1] + ls[2] * rel[2]
            along_t = lt[0] * rel[0] + lt[1] * rel[1] + lt[2] * rel[2]
            den_s = quad + len_s
            den_t = quad + len_t
            both = den_s * den_t
            near = pl.reciprocal(both, approx=True)
            near = near * (2.0 - both * near)
            half = 0.5 * near
            share_s = along_s * den_t * half
            share_t = along_t * den_s * half
            for k in range(3):
                skew = share_t * push[k]
                sums_t[k] = sums_t[k] + (push[k][0:8] + push[k][8:16])
                sums_t[k + 3] = sums_t[k + 3] - (skew[0:8] + skew[8:16])
            for k, value in enumerate(push + [share_s * push[k] for k in range(3)]):
                high, low = split(value)
                xs[slot, lo : lo + 16, 2 * k * LANES : (2 * k + 1) * LANES] = high
                xs[slot, lo : lo + 16, (2 * k + 1) * LANES : (2 * k + 2) * LANES] = low
        rows_t = empty
        for k in range(6):
            rows_t = jnp.where(sub == k, jnp.sum(sums_t[k], 0, keepdims=True), rows_t)
        rows_s = lax.dot_general(adder, xs[slot], (((1,), (1,)), ((), ())), preferred_element_type=F32)
        return rows_s, rows_t

    def several(q, _):
        group = [(slot, q * AT_ONCE + slot) for slot in range(AT_ONCE)]
        for slot, p in group:
            turn(slot, p)
        rows = [forces(slot, p) for slot, p in group]
        for slot, p in group:
            left, right = pairs[2 * p], pairs[2 * p + 1]
            acc[at_block(left), :] = acc[at_block(left), :] - rows[slot][0]
            acc[at_block(right), :] = acc[at_block(right), :] + rows[slot][1]
        return 0

    lax.fori_loop(0, (listed + AT_ONCE - 1) // AT_ONCE, several, 0)

    own_acc[...] = acc[0 : 8 * blocks]
    for r in range(4):
        lo = 8 * (blocks + r * width)
        ghost_acc[r] = acc[lo : lo + 8 * width]


def finish(width, slots, counts, own_acc, returned, far, out, acc):
    blocks = own_acc.shape[0] // 8
    acc[...] = own_acc[...] + far[...]
    for r in range(4):

        def add(g, _):
            at = at_block(slots[r * width + g])
            acc[at, :] = acc[at, :] + returned[r, at_block(g), :]
            return 0

        lax.fori_loop(0, counts[r], add, 0)

    def write(b, _):
        tile = acc[at_block(b), :]
        both = 0.5 * tile[0:3]
        out[0:3, at_lanes(b)] = both - tile[3:6]
        out[3:6, at_lanes(b)] = both + tile[3:6]
        return 0

    lax.fori_loop(0, blocks, write, 0, unroll=4)


def shape(*dims):
    return jax.ShapeDtypeStruct(dims, F32)


def on_device(sizes, ends, burgers, seg_cell, send_blocks, send_count, pair_list, pair_count):
    seg_here = ends.shape[1]
    blocks = seg_here // LANES
    width = send_blocks.shape[2]
    sent_rows = 9 * width
    (ax, nx), (ay, ny) = sizes
    slots = send_blocks.reshape(-1)
    counts = send_count.reshape(-1)
    cell = seg_cell.reshape(blocks, LANES)
    params = pltpu.CompilerParams(vmem_limit_bytes=VMEM_LIMIT)

    main, bz, terms, outgoing = pl.pallas_call(
        functools.partial(prepare, width),
        out_shape=(
            shape(blocks * 8, LANES),
            shape(blocks, LANES),
            shape(TERM_ROWS, seg_here),
            shape(4, sent_rows, LANES),
        ),
        in_specs=[SMEM_SPEC] * 2 + [VMEM_SPEC] * 2,
        out_specs=(VMEM_SPEC,) * 4,
        compiler_params=params,
        name="prepare",
    )(slots, counts, ends, burgers)

    dma = pltpu.SemaphoreType.DMA
    ghosts, moments = pl.pallas_call(
        functools.partial(exchange, sizes),
        out_shape=(shape(4, sent_rows, LANES), shape(TERM_ROWS, CELLS)),
        in_specs=[VMEM_SPEC] * 3,
        out_specs=(VMEM_SPEC,) * 2,
        scratch_shapes=[
            pltpu.VMEM((TERM_ROWS, CELLS), F32),
            pltpu.VMEM((nx - 1, TERM_ROWS, CELLS), F32),
            pltpu.VMEM((ny - 1, TERM_ROWS, CELLS), F32),
            pltpu.VMEM((TERM_ROWS, CELLS), F32),
            dma((4,)),
            dma((4,)),
            dma((nx - 1,)),
            dma((nx - 1,)),
            dma((ny - 1,)),
            dma((ny - 1,)),
        ],
        compiler_params=pltpu.CompilerParams(
            collective_id=0, has_side_effects=True, vmem_limit_bytes=VMEM_LIMIT
        ),
        name="exchange",
    )(outgoing, cell, terms)

    own_acc, ghost_acc = pl.pallas_call(
        functools.partial(interact, sizes, width),
        out_shape=(shape(blocks * 8, LANES), shape(4, 8 * width, LANES)),
        in_specs=[SMEM_SPEC] * 2 + [VMEM_SPEC] * 3,
        out_specs=(VMEM_SPEC,) * 2,
        scratch_shapes=[pltpu.VMEM(((blocks + 4 * width) * 8, LANES), F32)] * 3
        + [
            pltpu.VMEM((AT_ONCE, 80, 8 * LANES), BF16),
            pltpu.VMEM((AT_ONCE, LANES, 8 * LANES), F32),
            pltpu.VMEM((AT_ONCE, LANES, 12 * LANES), BF16),
        ],
        compiler_params=params,
        name="interact",
    )(pair_list.reshape(-1), pair_count, main, bz, ghosts)

    returned, far = pl.pallas_call(
        functools.partial(give_back, sizes),
        out_shape=(shape(4, 8 * width, LANES), shape(blocks * 8, LANES)),
        in_specs=[VMEM_SPEC] * 5,
        out_specs=(VMEM_SPEC,) * 2,
        scratch_shapes=[dma((4,)), dma((4,))],
        compiler_params=pltpu.CompilerParams(
            collective_id=1, has_side_effects=True, vmem_limit_bytes=VMEM_LIMIT
        ),
        name="give_back",
    )(ghost_acc, main, cell, terms, moments)

    return pl.pallas_call(
        functools.partial(finish, width),
        out_shape=shape(6, seg_here),
        in_specs=[SMEM_SPEC] * 2 + [VMEM_SPEC] * 3,
        out_specs=VMEM_SPEC,
        scratch_shapes=[pltpu.VMEM((blocks * 8, LANES), F32)],
        compiler_params=params,
        name="finish",
    )(slots, counts, own_acc, returned, far)


def solution(mesh):
    sizes = (("gx", mesh.shape["gx"]), ("gy", mesh.shape["gy"]))
    return jax.shard_map(
        functools.partial(on_device, sizes),
        mesh=mesh,
        in_specs=(
            P(None, ("gx", "gy")),
            P(None, ("gx", "gy")),
            P(("gx", "gy")),
            P(("gx", "gy"), None, None),
            P(("gx", "gy"), None),
            P(("gx", "gy"), None, None),
            P(),
        ),
        out_specs=P(None, ("gx", "gy")),
        check_vma=False,
    )
```
